512 devices in a mesh: rows: 32 (over x, z_hi, y), loop: 16 (over z_lo, core).
Axes of the slice: x: 4, y: 4, z: 16 (z_hi: 2, z_lo: 8; z = z_hi * 8 + z_lo), core: 2. Of those that a mesh axis runs over, the one named last changes fastest.
Arguments:
- integrals: float32 [2, 2, 8192, 8192], P(None, None, 'rows', 'loop'), may hold values from -6 to 6
- mask: int32 [2, 64, 64], P(None, 'rows', 'loop'), may hold values 0 or 1
- coeffs: float32 [8192, 640], P('loop'), may hold values from -0.0625 to 0.0625
Outputs:
- exchange: float32 [8192, 8192], P('rows', 'loop')
The draws below stay inside these ranges and needn't reach their ends.
All inputs are finite; a program needn't handle non-finite values. No bound on the sum of `mask` on one device may be relied on, other than what follows from the above.
Results may differ from the reference program's by a relative error of at most 0.00009.
Values sent between devices are 32-bit elements; how exact they have to be, the bound alone decides.
No kernel may reach another device: no remote copies, remote signals or barrier semaphores. Data moves between devices by JAX's collectives and lax.ppermute only.
A program may use at most 64 MiB of HBM per device.

```python
import jax
import jax.numpy as jnp
from jax import lax

NBF = 8192
NOCC = 640
TILE = 128
NSLAB = 2
AUX = 2


def plant(result, key, smallest, largest):
    index_at = [jax.random.randint(jax.random.fold_in(key, axis), (), 0, length) for axis, length in enumerate(result.shape)]
    longest = result.shape.index(max(result.shape))
    next_to = index_at[:longest] + [(index_at[longest] + 1) % result.shape[longest]] + index_at[longest + 1:]
    return result.at[tuple(index_at)].set(smallest).at[tuple(next_to)].set(largest)


def shard_levels(own_key, shape, split, low, largest):
    gain, own = 1.0, jax.random.fold_in(own_key, 6)
    for dim, blocks in split:
        draws = jnp.exp(jax.random.uniform(jax.random.fold_in(own, dim), (blocks,), jnp.float32, low / len(split), largest / len(split)))
        gain = gain * jnp.repeat(draws, shape[dim] // blocks).reshape([-1 if axis == dim else 1 for axis in range(len(shape))])
    return gain


def normal_values(key, extent, width, most, split=(), dtype=jnp.bfloat16):
    result = jax.random.normal(key, extent, jnp.float32) * width
    if len(split) > 0:
        result = shard_levels(key, extent, split, -0.22, 0.18) * result
    return jnp.clip(result, min=-most, max=most).astype(dtype)


def setup_inputs(seed: int = 0) -> dict:
    arg_keys = jax.random.split(jax.random.key(seed), 4)
    integrals = normal_values(arg_keys[0], (NSLAB, AUX, NBF, NBF), 1.0, 6.0, ((2, 32), (3, 16)), jnp.float32)
    mask = plant((jax.random.randint(arg_keys[1], (NSLAB, NBF // TILE, NBF // TILE), 0, 2) < 1).astype(jnp.int32), jax.random.fold_in(arg_keys[1], 1), 0, 1)
    coeffs = normal_values(arg_keys[2], (NBF, NOCC), NBF ** -0.5, 0.0625, ((0, 16),), jnp.float32)
    return {"integrals": integrals, "mask": mask, "coeffs": coeffs}


def reference(integrals, mask, coeffs):
    blocks = mask.astype(jnp.float32)[:, None, :, None, :, None]
    shaped = integrals.reshape(NSLAB, AUX, NBF // TILE, TILE, NBF // TILE, TILE)
    masked = (shaped * blocks).reshape(NSLAB * AUX, NBF, NBF)
    half = jnp.einsum('pml,li->ipm', masked, coeffs, precision=lax.Precision.HIGHEST)
    scale = 1.0 / jnp.sqrt(jnp.float32(NSLAB * AUX * NOCC))
    total = jnp.einsum('ipm,ipn->mn', half, half, precision=lax.Precision.HIGHEST)
    return (total * scale).astype(jnp.float32)
```

```python
import jax
import jax.numpy as jnp
from jax import lax
from jax.experimental import pallas as pl
from jax.experimental.pallas import tpu as pltpu
from jax.sharding import Mesh, PartitionSpec as P

TILE = 128
VMEM = 48 * 1024 * 1024
HANDED = ((0, 3, 1, 2, 2, 1, 3, 0), (3, 0, 2, 1, 1, 2, 0, 3))
NT = (((1,), (1,)), ((), ()))


def halves(value):
    high = value.astype(jnp.bfloat16)
    return high, (value - high.astype(jnp.float32)).astype(jnp.bfloat16)


def half_kernel(slab_ref, mask_ref, a_ref, c_ref, o_ref, chigh, clow, ahigh, alow):
    @pl.when(pl.program_id(0) == 0)
    def _():
        chigh[...], clow[...] = halves(c_ref[...])

    slab = slab_ref[0]
    for i in range(a_ref.shape[2] // TILE):
        for j in range(a_ref.shape[3] // TILE):
            at = (pl.ds(i * TILE, TILE), pl.ds(j * TILE, TILE))
            kept = mask_ref[slab, i, j].astype(jnp.float32)
            ahigh[at], alow[at] = halves(a_ref[0, 0, at[0], at[1]] * kept)
    dot = lambda a, b: jnp.dot(a, b, preferred_element_type=jnp.float32)
    o_ref[0] = dot(ahigh[...], chigh[...]) + (dot(ahigh[...], clow[...]) + dot(alow[...], chigh[...]))


def half_of_slab(integrals, mask, coeffs, slab):
    nslab, naux, mrows, lcols = integrals.shape
    norbit = coeffs.shape[1]
    return pl.pallas_call(
        half_kernel,
        out_shape=jax.ShapeDtypeStruct((naux, mrows, norbit), jnp.float32),
        grid_spec=pltpu.PrefetchScalarGridSpec(
            num_scalar_prefetch=2,
            grid=(naux,),
            in_specs=[
                pl.BlockSpec((1, 1, mrows, lcols), lambda a, slab, mask: (slab[0], a, 0, 0)),
                pl.BlockSpec((lcols, norbit), lambda a, slab, mask: (0, 0)),
            ],
            out_specs=pl.BlockSpec((1, mrows, norbit), lambda a, slab, mask: (a, 0, 0)),
            scratch_shapes=[pltpu.VMEM((lcols, norbit), jnp.bfloat16)] * 2
            + [pltpu.VMEM((mrows, lcols), jnp.bfloat16)] * 2,
        ),
        compiler_params=pltpu.CompilerParams(vmem_limit_bytes=VMEM),
        cost_estimate=pl.CostEstimate(flops=6 * naux * mrows * lcols * norbit, bytes_accessed=4 * naux * mrows * (lcols + norbit) + 4 * lcols * norbit, transcendentals=0),
    )(slab.reshape(1), mask, integrals, coeffs)


def exchange_kernel(m_ref, n_ref, o_ref, mhigh, mlow, nhigh, nlow):
    planes, naux, rows, norbit = m_ref.shape
    parts, _, _, sub, _ = n_ref.shape
    per = parts // naux

    @pl.when(pl.program_id(0) == 0)
    def _():
        for a in range(naux):
            for z in range(planes):
                at = pl.ds(z * rows, rows)
                mhigh[a, at, :], mlow[a, at, :] = halves(m_ref[z, a])

    total = None
    for a in range(naux):
        for h in range(per):
            for z in range(planes):
                at = pl.ds(z * rows + h * sub, sub)
                nhigh[a, at, :], nlow[a, at, :] = halves(n_ref[a * per + h, 0, z])
        dot = lambda l, r: lax.dot_general(l[a], r[a], NT, preferred_element_type=jnp.float32)
        term = dot(mhigh, nhigh) + (dot(mhigh, nlow) + dot(mlow, nhigh))
        total = term if total is None else total + term
    o_ref[0] = total


def exchange_part(m, n):
    planes, naux, rows, norbit = m.shape
    parts, blocks, _, sub, _ = n.shape
    mrows = planes * rows
    return pl.pallas_call(
        exchange_kernel,
        out_shape=jax.ShapeDtypeStruct((blocks, mrows, mrows), jnp.float32),
        grid=(blocks,),
        in_specs=[
            pl.BlockSpec(m.shape, lambda y: (0, 0, 0, 0)),
            pl.BlockSpec((parts, 1, planes, sub, norbit), lambda y: (0, y, 0, 0, 0)),
        ],
        out_specs=pl.BlockSpec((1, mrows, mrows), lambda y: (y, 0, 0)),
        scratch_shapes=[pltpu.VMEM((naux, mrows, norbit), jnp.bfloat16)] * 4,
        compiler_params=pltpu.CompilerParams(vmem_limit_bytes=VMEM),
        cost_estimate=pl.CostEstimate(flops=6 * naux * blocks * mrows * mrows * norbit, bytes_accessed=4 * naux * mrows * norbit * (blocks + 1) + 4 * blocks * mrows * mrows, transcendentals=0),
    )(m, n)


def swap(value, axis, bit, size):
    return lax.ppermute(value, axis, [(i, i ^ bit) for i in range(size)])


def pick(value, index, axis):
    return lax.dynamic_index_in_dim(value, index, axis, keepdims=False)


def local(integrals, mask, coeffs):
    nslab, naux, mrows, lcols = integrals.shape
    norbit = coeffs.shape[1]
    core, zl, zh = lax.axis_index("core"), lax.axis_index("zl"), lax.axis_index("zh")
    rows = mrows // 8
    away = half_of_slab(integrals, mask, coeffs, 1 - core)
    kept = half_of_slab(integrals, mask, coeffs, core)
    part = kept + swap(away, "core", 1, 2)
    part = part.reshape(naux, 4, 2, rows, norbit)
    part = pick(part, zl & 1, 2) + swap(pick(part, 1 - (zl & 1), 2), "zl", 1, 8)
    part = part.reshape(naux, 2, 2, rows, norbit)
    bit = (zl >> 1) & 1
    part = pick(part, bit, 2) + swap(pick(part, 1 - bit, 2), "zl", 2, 8)
    bit = zl >> 2
    own = pick(part, bit, 1) + swap(pick(part, 1 - bit, 1), "zl", 4, 8)
    m = lax.all_gather(own, "zl")
    sub = rows // 2
    pieces = lax.all_to_all(own.reshape(2 * naux, sub, norbit), "x", split_axis=0, concat_axis=0)
    handed = jnp.stack([jnp.where(zh == 0, pieces[a], pieces[b]) for a, b in zip(*HANDED)])
    moved = lax.all_to_all(handed, "zl", split_axis=0, concat_axis=0)
    mirror = [(z, 15 - z) for z in range(16) if z % 2 == (z < 8)]
    passed = lax.ppermute(moved, ("zh", "zl"), mirror)
    mine = jnp.where(zh == (zl & 1), moved, passed)
    copies = jnp.broadcast_to(mine[None], (16,) + mine.shape)
    n = lax.all_to_all(copies, ("x", "y"), split_axis=0, concat_axis=0)
    n = n.reshape(4, 4, 8, sub, norbit)
    partial = exchange_part(m, n).reshape(2, 2, mrows, mrows)
    total = pick(partial, core, 0) + swap(pick(partial, 1 - core, 0), "core", 1, 2)
    total = jnp.swapaxes(total, 0, 1).reshape(mrows, lcols)
    return total * (1.0 / jnp.sqrt(jnp.float32(norbit * nslab * naux)))


def solution(mesh):
    fine = Mesh(mesh.devices.reshape(4, 2, 4, 8, 2), ("x", "zh", "y", "zl", "core"))
    r, c = ("x", "zh", "y"), ("zl", "core")
    in_specs = (P(None, None, r, c), P(None, r, c), P(c, None))
    return jax.shard_map(local, mesh=fine, in_specs=in_specs, out_specs=P(r, c), check_vma=False)
```

```python
import jax
import jax.numpy as jnp
from jax import lax
from jax.experimental import pallas as pl
from jax.experimental.pallas import tpu as pltpu
from jax.sharding import Mesh, PartitionSpec as P

TILE = 128
VMEM = 60 * 1024 * 1024
NT = (((1,), (1,)), ((), ()))


def halves(value):
    high = value.astype(jnp.bfloat16)
    return high, (value - high.astype(jnp.float32)).astype(jnp.bfloat16)


def dot(a, b, dims=(((1,), (0,)), ((), ()))):
    return lax.dot_general(a, b, dims, preferred_element_type=jnp.float32)


def split_kernel(c_ref, high_ref, low_ref):
    high_ref[...], low_ref[...] = halves(c_ref[...])


def split(value):
    half = jax.ShapeDtypeStruct(value.shape, jnp.bfloat16)
    return pl.pallas_call(split_kernel, out_shape=(half, half))(value)


def half_kernel(slab_ref, mask_ref, a_ref, chigh_ref, clow_ref, o_ref, ahigh, alow):
    slab = slab_ref[0]
    for i in range(a_ref.shape[2] // TILE):
        for j in range(a_ref.shape[3] // TILE):
            at = (pl.ds(i * TILE, TILE), pl.ds(j * TILE, TILE))
            kept = mask_ref[slab, i, j].astype(jnp.float32)
            ahigh[at], alow[at] = halves(a_ref[0, 0, at[0], at[1]] * kept)
    chigh = chigh_ref[...]
    o_ref[...] = dot(ahigh[...], chigh) + (dot(ahigh[...], clow_ref[...]) + dot(alow[...], chigh))


def half_of(integrals, mask, chigh, clow, slab, aux):
    _, _, mrows, lcols = integrals.shape
    norbit = chigh.shape[1]
    return pl.pallas_call(
        half_kernel,
        out_shape=jax.ShapeDtypeStruct((mrows, norbit), jnp.float32),
        grid_spec=pltpu.PrefetchScalarGridSpec(
            num_scalar_prefetch=2,
            grid=(1,),
            in_specs=[
                pl.BlockSpec((1, 1, mrows, lcols), lambda g, slab, mask: (slab[0], aux, 0, 0)),
                pl.BlockSpec((lcols, norbit), lambda g, slab, mask: (0, 0)),
                pl.BlockSpec((lcols, norbit), lambda g, slab, mask: (0, 0)),
            ],
            out_specs=pl.BlockSpec((mrows, norbit), lambda g, slab, mask: (0, 0)),
            scratch_shapes=[pltpu.VMEM((mrows, lcols), jnp.bfloat16)] * 2,
        ),
        compiler_params=pltpu.CompilerParams(vmem_limit_bytes=VMEM),
        cost_estimate=pl.CostEstimate(flops=6 * mrows * lcols * norbit, bytes_accessed=4 * mrows * (lcols + norbit) + 4 * lcols * norbit, transcendentals=0),
    )(slab.reshape(1), mask, integrals, chigh, clow)


def exchange_kernel(place_ref, m_ref, n_ref, o_ref, mhigh, mlow, nhigh, nlow):
    planes, naux, rows, norbit = m_ref.shape
    parts, _, _, _, sub, _ = n_ref.shape
    per = parts // naux

    @pl.when(pl.program_id(0) == 0)
    def _():
        for z in range(planes):
            at = pl.ds(pl.multiple_of(place_ref[1 + z] * rows, rows), rows)
            for a in range(naux):
                mhigh[a, at, :], mlow[a, at, :] = halves(m_ref[z, a])

    total = None
    for a in range(naux):
        for h in range(per):
            for z in range(planes):
                at = pl.ds(z * rows + h * 2 * sub, 2 * sub)
                both = jnp.concatenate([n_ref[a * per + h, 0, k, z] for k in range(2)], axis=0)
                nhigh[a, at, :], nlow[a, at, :] = halves(both)
        term = dot(mhigh[a], nhigh[a], NT) + (dot(mhigh[a], nlow[a], NT) + dot(mlow[a], nhigh[a], NT))
        total = term if total is None else total + term
    o_ref[...] = total


def exchange_part(m, n, place):
    planes, naux, rows, norbit = m.shape
    parts, blocks, _, _, sub, _ = n.shape
    mrows = planes * rows
    mine = blocks // 2
    return pl.pallas_call(
        exchange_kernel,
        out_shape=jax.ShapeDtypeStruct((mrows, mine * mrows), jnp.float32),
        grid_spec=pltpu.PrefetchScalarGridSpec(
            num_scalar_prefetch=1,
            grid=(mine,),
            in_specs=[
                pl.BlockSpec(m.shape, lambda y, place: (0, 0, 0, 0)),
                pl.BlockSpec((parts, 1, 2, planes, sub, norbit), lambda y, place: (0, place[0] * mine + y, 0, 0, 0, 0)),
            ],
            out_specs=pl.BlockSpec((mrows, mrows), lambda y, place: (0, y)),
            scratch_shapes=[pltpu.VMEM((naux, mrows, norbit), jnp.bfloat16)] * 4,
        ),
        compiler_params=pltpu.CompilerParams(vmem_limit_bytes=VMEM),
        cost_estimate=pl.CostEstimate(flops=6 * naux * mine * mrows * mrows * norbit, bytes_accessed=4 * naux * mrows * norbit * (mine + 1) + 4 * mine * mrows * mrows, transcendentals=0),
    )(place, m, n)


def swap(value, axis, bit, size):
    return lax.ppermute(value, axis, [(i, i ^ bit) for i in range(size)])


def pick(value, index, axis):
    return lax.dynamic_index_in_dim(value, index, axis, keepdims=False)


def local(integrals, mask, coeffs):
    nslab, naux, mrows, lcols = integrals.shape
    norbit = coeffs.shape[1]
    core, zl, zh = lax.axis_index("core"), lax.axis_index("zl"), lax.axis_index("zh")
    rows = mrows // 8
    low, mid, top = zl & 1, (zl >> 1) & 1, zl >> 2
    chigh, clow = split(coeffs)
    chunks = range(naux)
    away = [half_of(integrals, mask, chigh, clow, 1 - core, a) for a in chunks]
    got = [swap(away[a], "core", 1, 2) for a in chunks]
    kept = [half_of(integrals, mask, chigh, clow, core, a) for a in chunks]
    part = [(kept[a].reshape(4, 2, rows, norbit), got[a].reshape(4, 2, rows, norbit)) for a in chunks]
    give = [pick(k, 1 - low, 1) + pick(g, 1 - low, 1) for k, g in part]
    keep = [pick(k, low, 1) + pick(g, low, 1) for k, g in part]
    part = [(k.reshape(2, 2, rows, norbit), swap(g, "zl", 1, 8).reshape(2, 2, rows, norbit)) for k, g in zip(keep, give)]
    give = [pick(k, 1 - mid, 1) + pick(g, 1 - mid, 1) for k, g in part]
    keep = [pick(k, mid, 1) + pick(g, mid, 1) for k, g in part]
    part = [(k, swap(g, "zl", 2, 8)) for k, g in zip(keep, give)]
    give = [pick(k, 1 - top, 0) + pick(g, 1 - top, 0) for k, g in part]
    keep = [pick(k, top, 0) + pick(g, top, 0) for k, g in part]
    own = jnp.stack([k + swap(g, "zl", 4, 8) for k, g in zip(keep, give)])
    sub = rows // 4
    pieces = lax.all_to_all(own.reshape(2 * naux, 2 * sub, norbit), "x", split_axis=0, concat_axis=0)
    pieces = pieces.reshape(4, 2, sub, norbit)
    handed = jnp.where(zh == 0, pieces, pieces[:, ::-1]).reshape(1, 8, sub, norbit)
    handed = jnp.broadcast_to(handed, (2, 8, sub, norbit)).reshape(16, sub, norbit)
    moved = lax.all_to_all(handed, ("zh", "zl"), split_axis=0, concat_axis=0).reshape(2, 8, sub, norbit)
    other = swap(pick(moved, 1 - low, 0), "zl", 1, 8)
    mine = jnp.stack([pick(moved, low, 0), other])
    copies = jnp.broadcast_to(mine[None], (16,) + mine.shape)
    n = lax.all_to_all(copies, ("x", "y"), split_axis=0, concat_axis=0)
    n = n.reshape(4, 4, 2, 8, sub, norbit)
    m = own[None]
    order = [0]
    for bit in (4, 2, 1):
        m = jnp.concatenate([m, swap(m, "zl", bit, 8)])
        order = order + [k ^ bit for k in order]
    planes = [zl ^ k for k in order]
    sent = exchange_part(m, n, jnp.stack([1 - core] + planes))
    held = exchange_part(m, n, jnp.stack([core] + planes))
    return (held + swap(sent, "core", 1, 2)) * (1.0 / jnp.sqrt(jnp.float32(norbit * nslab * naux)))


def solution(mesh):
    fine = Mesh(mesh.devices.reshape(4, 2, 4, 8, 2), ("x", "zh", "y", "zl", "core"))
    r, c = ("x", "zh", "y"), ("zl", "core")
    in_specs = (P(None, None, r, c), P(None, r, c), P(c, None))
    return jax.shard_map(local, mesh=fine, in_specs=in_specs, out_specs=P(r, c), check_vma=False)
```

```python
import jax
import jax.numpy as jnp
from jax import lax
from jax.experimental import pallas as pl
from jax.experimental.pallas import tpu as pltpu
from jax.sharding import Mesh, PartitionSpec as P

TILE = 128
VMEM = 60 * 1024 * 1024
NT = (((1,), (1,)), ((), ()))


def halves(value):
    high = value.astype(jnp.bfloat16)
    return high, (value - high.astype(jnp.float32)).astype(jnp.bfloat16)


def dot(a, b, dims=(((1,), (0,)), ((), ()))):
    return lax.dot_general(a, b, dims, preferred_element_type=jnp.float32)


def half_kernel(half_ref, mask_ref, a_ref, c_ref, *rest):
    *o_refs, chigh, clow, ahigh, alow = rest
    chunk = pl.program_id(0)
    parts, rows, lcols = a_ref.shape

    @pl.when(chunk == 0)
    def _():
        chigh[...], clow[...] = halves(c_ref[...])

    for p in range(parts):
        for j in range(lcols // TILE):
            at = (pl.ds(p * rows, rows), pl.ds(j * TILE, TILE))
            kept = mask_ref[p * mask_ref.shape[0] // parts, half_ref[0], j].astype(jnp.float32)
            ahigh[at], alow[at] = halves(a_ref[p, :, at[1]] * kept)
    total = dot(ahigh[...], chigh[...]) + (dot(ahigh[...], clow[...]) + dot(alow[...], chigh[...]))
    for k, o_ref in enumerate(o_refs):
        @pl.when(chunk == k)
        def _():
            o_ref[...] = total.reshape(o_ref.shape)


def half_of(integrals, mask, coeffs, half):
    parts, mrows, lcols = integrals.shape
    norbit = coeffs.shape[1]
    rows = mrows // 4
    return pl.pallas_call(
        half_kernel,
        out_shape=[jax.ShapeDtypeStruct((parts, rows, norbit), jnp.float32)] * 2,
        grid_spec=pltpu.PrefetchScalarGridSpec(
            num_scalar_prefetch=2,
            grid=(2,),
            in_specs=[
                pl.BlockSpec((parts, rows, lcols), lambda k, half, mask: (0, half[0] * 2 + k, 0)),
                pl.BlockSpec((lcols, norbit), lambda k, half, mask: (0, 0)),
            ],
            out_specs=[pl.BlockSpec((parts, rows, norbit), lambda k, half, mask: (0, 0, 0))] * 2,
            scratch_shapes=[pltpu.VMEM((lcols, norbit), jnp.bfloat16)] * 2
            + [pltpu.VMEM((parts * rows, lcols), jnp.bfloat16)] * 2,
        ),
        compiler_params=pltpu.CompilerParams(vmem_limit_bytes=VMEM),
        cost_estimate=pl.CostEstimate(flops=3 * parts * mrows * lcols * norbit, bytes_accessed=2 * parts * mrows * (lcols + norbit) + 4 * lcols * norbit, transcendentals=0),
    )(half.reshape(1), mask, integrals, coeffs)


def exchange_kernel(core_ref, mown_ref, moth_ref, nown_ref, noth_ref, o_ref, mhigh, mlow, nhigh, nlow):
    chunks, _, rows, norbit = mown_ref.shape
    blocks = nown_ref.shape[0]
    own = pl.multiple_of(core_ref[0] * chunks * rows, chunks * rows)
    oth = pl.multiple_of((1 - core_ref[0]) * chunks * rows, chunks * rows)

    @pl.when(pl.program_id(0) == 0)
    def _():
        for y in range(blocks):
            for k in range(chunks):
                for start, ref in ((own, nown_ref), (oth, noth_ref)):
                    at = pl.ds(start + (y * 2 * chunks + k) * rows, rows)
                    nhigh[at, :], nlow[at, :] = halves(ref[y, k])

    for k in range(chunks):
        for start, ref in ((own, mown_ref), (oth, moth_ref)):
            at = pl.ds(start + k * rows, rows)
            mhigh[at, :], mlow[at, :] = halves(ref[k, 0])
    o_ref[0] = dot(mhigh[...], nhigh[...], NT) + (dot(mhigh[...], nlow[...], NT) + dot(mlow[...], nhigh[...], NT))


def exchange_part(mown, moth, nown, noth, core):
    chunks, parts, rows, norbit = mown.shape
    blocks = nown.shape[0]
    mrows, ncols = 2 * chunks * rows, blocks * 2 * chunks * rows
    mspec = pl.BlockSpec((chunks, 1, rows, norbit), lambda x, core: (0, x, 0, 0))
    nspec = pl.BlockSpec(nown.shape, lambda x, core: (0, 0, 0, 0))
    return pl.pallas_call(
        exchange_kernel,
        out_shape=jax.ShapeDtypeStruct((parts, mrows, ncols), jnp.float32),
        grid_spec=pltpu.PrefetchScalarGridSpec(
            num_scalar_prefetch=1,
            grid=(parts,),
            in_specs=[mspec, mspec, nspec, nspec],
            out_specs=pl.BlockSpec((1, mrows, ncols), lambda x, core: (x, 0, 0)),
            scratch_shapes=[pltpu.VMEM((mrows, norbit), jnp.bfloat16)] * 2 + [pltpu.VMEM((ncols, norbit), jnp.bfloat16)] * 2,
        ),
        compiler_params=pltpu.CompilerParams(vmem_limit_bytes=VMEM),
        cost_estimate=pl.CostEstimate(flops=6 * parts * mrows * ncols * norbit, bytes_accessed=4 * norbit * (parts * mrows + ncols) + 4 * parts * mrows * ncols, transcendentals=0),
    )(core.reshape(1), mown, moth, nown, noth)


def swap(value, axis, bit, size):
    return lax.ppermute(value, axis, [(i, i ^ bit) for i in range(size)])


def pick(value, index, axis):
    return lax.dynamic_index_in_dim(value, index, axis, keepdims=False)


def join(own, got, bit, axis):
    return jnp.stack([jnp.where(bit == 0, own, got), jnp.where(bit == 0, got, own)], axis=axis)


def local(integrals, mask, coeffs):
    nslab, naux, mrows, lcols = integrals.shape
    norbit = coeffs.shape[1]
    core, zl, zh = lax.axis_index("core"), lax.axis_index("zl"), lax.axis_index("zh")
    low, mid = zl & 1, (zl >> 1) & 1
    parts = nslab * naux
    sub = mrows // 32
    chunks = (0, 1)
    integrals = integrals.reshape(parts, mrows, lcols)
    away = half_of(integrals, mask, coeffs, 1 - core)
    got = [swap(a, "core", 1, 2) for a in away]
    kept = half_of(integrals, mask, coeffs, core)
    part = [(v.reshape(parts, 2, 2, 2, sub, norbit), g.reshape(parts, 2, 2, 2, sub, norbit)) for v, g in zip(kept, got)]
    give = [pick(v, 1 - low, 3) + pick(g, 1 - low, 3) for v, g in part]
    keep = [pick(v, low, 3) + pick(g, low, 3) for v, g in part]
    part = [(v, swap(g, "zl", 1, 8)) for v, g in zip(keep, give)]
    give = [pick(v, 1 - mid, 2) + pick(g, 1 - mid, 2) for v, g in part]
    keep = [pick(v, mid, 2) + pick(g, mid, 2) for v, g in part]
    part = jnp.stack([v + swap(g, "zl", 2, 8) for v, g in zip(keep, give)], axis=1)
    part = lax.all_to_all(part, "x", split_axis=0, concat_axis=0)
    rows = []
    for k in chunks:
        m = part[:, k]
        m = m + swap(m, "zl", 4, 8)
        m = join(m, swap(m, "zl", 2, 8), mid, 2)
        m = join(m, swap(m, "zl", 1, 8), low, 3)
        rows.append(m.reshape(4, 8 * sub, norbit))
    mirror = [(z, 15 - z) for z in range(16) if z % 2 == (z < 8)]
    cols = []
    for m in rows:
        passed = lax.ppermute(pick(m, 3 - (zl >> 1), 0), ("zh", "zl"), mirror)
        cols.append(jnp.where(zh == low, pick(m, zl >> 1, 0), passed))
    cols = jnp.stack(cols)
    m = jnp.stack(rows)
    moth = swap(m, "core", 1, 2)
    n = lax.all_to_all(jnp.broadcast_to(cols[None], (4,) + cols.shape), "y", split_axis=0, concat_axis=0)
    n = n.reshape((2, 2) + cols.shape)
    nown, noth = pick(n, core, 0), swap(pick(n, 1 - core, 0), "core", 1, 2)
    partial = exchange_part(m, moth, nown, noth, core)
    partial = lax.all_to_all(partial, "x", split_axis=0, concat_axis=0)
    return jnp.sum(partial, axis=0) * (1.0 / jnp.sqrt(jnp.float32(norbit * parts)))


def solution(mesh):
    fine = Mesh(mesh.devices.reshape(4, 2, 4, 8, 2), ("x", "zh", "y", "zl", "core"))
    r, c = ("x", "zh", "y"), ("zl", "core")
    in_specs = (P(None, None, r, c), P(None, r, c), P(c, None))
    return jax.shard_map(local, mesh=fine, in_specs=in_specs, out_specs=P(r, c), check_vma=False)
```

```python
import jax
import jax.numpy as jnp
from jax import lax
from jax.experimental import pallas as pl
from jax.experimental.pallas import tpu as pltpu
from jax.sharding import Mesh, PartitionSpec as P

TILE = 128
VMEM = 60 * 1024 * 1024
NT = (((1,), (1,)), ((), ()))


def halves(value):
    high = value.astype(jnp.bfloat16)
    return high, (value - high.astype(jnp.float32)).astype(jnp.bfloat16)


def dot(a, b, dims=(((1,), (0,)), ((), ()))):
    return lax.dot_general(a, b, dims, preferred_element_type=jnp.float32)


def half_kernel(slab_ref, mask_ref, a_ref, c_ref, *rest):
    *o_refs, chigh, clow, ahigh, alow = rest
    aux = pl.program_id(0)

    @pl.when(aux == 0)
    def _():
        chigh[...], clow[...] = halves(c_ref[...])

    slab = slab_ref[0]
    for i in range(a_ref.shape[2] // TILE):
        for j in range(a_ref.shape[3] // TILE):
            at = (pl.ds(i * TILE, TILE), pl.ds(j * TILE, TILE))
            kept = mask_ref[slab, i, j].astype(jnp.float32)
            ahigh[at], alow[at] = halves(a_ref[0, 0, at[0], at[1]] * kept)
    total = dot(ahigh[...], chigh[...]) + (dot(ahigh[...], clow[...]) + dot(alow[...], chigh[...]))
    for k, o_ref in enumerate(o_refs):
        @pl.when(aux == k)
        def _():
            o_ref[...] = total


def half_of(integrals, mask, coeffs, slab):
    _, naux, mrows, lcols = integrals.shape
    norbit = coeffs.shape[1]
    return pl.pallas_call(
        half_kernel,
        out_shape=[jax.ShapeDtypeStruct((mrows, norbit), jnp.float32)] * naux,
        grid_spec=pltpu.PrefetchScalarGridSpec(
            num_scalar_prefetch=2,
            grid=(naux,),
            in_specs=[
                pl.BlockSpec((1, 1, mrows, lcols), lambda a, slab, mask: (slab[0], a, 0, 0)),
                pl.BlockSpec((lcols, norbit), lambda a, slab, mask: (0, 0)),
            ],
            out_specs=[pl.BlockSpec((mrows, norbit), lambda a, slab, mask: (0, 0))] * naux,
            scratch_shapes=[pltpu.VMEM((lcols, norbit), jnp.bfloat16)] * 2
            + [pltpu.VMEM((mrows, lcols), jnp.bfloat16)] * 2,
        ),
        compiler_params=pltpu.CompilerParams(vmem_limit_bytes=VMEM),
        cost_estimate=pl.CostEstimate(flops=6 * naux * mrows * lcols * norbit, bytes_accessed=4 * naux * mrows * (lcols + norbit) + 4 * lcols * norbit, transcendentals=0),
    )(slab.reshape(1), mask, integrals, coeffs)


def exchange_kernel(place_ref, m_ref, n_ref, sent_ref, held_ref, mhigh, mlow, nhigh, nlow):
    lanes, naux, tops, rows, norbit = m_ref.shape
    sub = n_ref.shape[5]
    step = pl.program_id(0)

    @pl.when(step == 0)
    def _():
        for lane in range(lanes):
            for top in range(tops):
                at = pl.ds(pl.multiple_of((top * lanes + place_ref[1 + lane]) * rows, rows), rows)
                for a in range(naux):
                    mhigh[a, at, :], mlow[a, at, :] = halves(m_ref[lane, a, top])

    total = None
    for a in range(naux):
        for h in range(2):
            for top in range(tops):
                for lane in range(lanes):
                    at = pl.ds((top * lanes + lane) * rows + h * 2 * sub, 2 * sub)
                    both = jnp.concatenate([n_ref[a * 2 + h, 0, k, lane, top] for k in range(2)], axis=0)
                    nhigh[a, at, :], nlow[a, at, :] = halves(both)
        term = dot(mhigh[a], nhigh[a], NT) + (dot(mhigh[a], nlow[a], NT) + dot(mlow[a], nhigh[a], NT))
        total = term if total is None else total + term

    @pl.when(step < 2)
    def _():
        sent_ref[...] = total

    @pl.when(step >= 2)
    def _():
        held_ref[...] = total


def exchange_part(m, n, place):
    lanes, naux, tops, rows, norbit = m.shape
    blocks = n.shape[1]
    mrows = lanes * tops * rows
    half = jax.ShapeDtypeStruct((mrows, blocks // 2 * mrows), jnp.float32)
    return pl.pallas_call(
        exchange_kernel,
        out_shape=(half, half),
        grid_spec=pltpu.PrefetchScalarGridSpec(
            num_scalar_prefetch=1,
            grid=(blocks,),
            in_specs=[
                pl.BlockSpec(m.shape, lambda g, place: (0,) * 5),
                pl.BlockSpec(n.shape[:1] + (1,) + n.shape[2:], lambda g, place: (0, (g + 2 * (1 - place[0])) % 4, 0, 0, 0, 0, 0)),
            ],
            out_specs=(
                pl.BlockSpec((mrows, mrows), lambda g, place: (0, jnp.minimum(g, 1))),
                pl.BlockSpec((mrows, mrows), lambda g, place: (0, jnp.maximum(g - 2, 0))),
            ),
            scratch_shapes=[pltpu.VMEM((naux, mrows, norbit), jnp.bfloat16)] * 4,
        ),
        compiler_params=pltpu.CompilerParams(vmem_limit_bytes=VMEM),
        cost_estimate=pl.CostEstimate(flops=6 * naux * blocks * mrows * mrows * norbit, bytes_accessed=4 * naux * mrows * norbit * (blocks + 1) + 4 * blocks * mrows * mrows, transcendentals=0),
    )(place, m, n)


def swap(value, axis, bit, size):
    return lax.ppermute(value, axis, [(i, i ^ bit) for i in range(size)])


def pick(value, index, axis):
    return lax.dynamic_index_in_dim(value, index, axis, keepdims=False)


def local(integrals, mask, coeffs):
    nslab, naux, mrows, lcols = integrals.shape
    norbit = coeffs.shape[1]
    core, zl, zh = lax.axis_index("core"), lax.axis_index("zl"), lax.axis_index("zh")
    rows, sub = mrows // 8, mrows // 32
    low, mid = zl & 1, (zl >> 1) & 1
    away = half_of(integrals, mask, coeffs, 1 - core)
    got = [swap(a, "core", 1, 2) for a in away]
    kept = half_of(integrals, mask, coeffs, core)
    part = [(k.reshape(4, 2, rows, norbit), g.reshape(4, 2, rows, norbit)) for k, g in zip(kept, got)]
    give = [pick(k, 1 - low, 1) + pick(g, 1 - low, 1) for k, g in part]
    keep = [pick(k, low, 1) + pick(g, low, 1) for k, g in part]
    part = [(k.reshape(2, 2, rows, norbit), swap(g, "zl", 1, 8).reshape(2, 2, rows, norbit)) for k, g in zip(keep, give)]
    give = [pick(k, 1 - mid, 1) + pick(g, 1 - mid, 1) for k, g in part]
    keep = [pick(k, mid, 1) + pick(g, mid, 1) for k, g in part]
    m = jnp.stack([k + swap(g, "zl", 2, 8) for k, g in zip(keep, give)])
    pieces = jnp.swapaxes(m.reshape(naux, 2, 2, 2 * sub, norbit), 1, 2).reshape(2 * naux, 2, 2 * sub, norbit)
    pieces = lax.all_to_all(pieces, "x", split_axis=0, concat_axis=0)
    pieces = jnp.swapaxes(pieces.reshape(4, 2, 2, sub, norbit), 1, 2)
    handed = jnp.where(zh == 0, pieces, pieces[:, ::-1]).reshape(1, 8, 2, sub, norbit)
    handed = jnp.broadcast_to(handed, (2, 8, 2, sub, norbit)).reshape(16, 2, sub, norbit)
    moved = lax.all_to_all(handed, ("zh", "zl"), split_axis=0, concat_axis=0).reshape(2, 2, 4, 2, sub, norbit)
    other = pick(moved, 1 - low, 0)
    other = swap(other[0] + other[1], "zl", 1, 8)
    moved = pick(moved, low, 0)
    mine = jnp.stack([moved[0] + moved[1], other])
    m, mine = lax.optimization_barrier((m, mine))
    copies = jnp.broadcast_to(mine[None], (16,) + mine.shape)
    n = lax.all_to_all(copies, ("x", "y"), split_axis=0, concat_axis=0)
    n = n.reshape((4, 4) + mine.shape)
    m = (m + swap(m, "zl", 4, 8))[None]
    order = [0]
    for bit in (2, 1):
        m = jnp.concatenate([m, swap(m, "zl", bit, 8)])
        order = order + [k ^ bit for k in order]
    sent, held = exchange_part(m, n, jnp.stack([core] + [(zl ^ k) & 3 for k in order]))
    return (held + swap(sent, "core", 1, 2)) * (1.0 / jnp.sqrt(jnp.float32(norbit * nslab * naux)))


def solution(mesh):
    fine = Mesh(mesh.devices.reshape(4, 2, 4, 8, 2), ("x", "zh", "y", "zl", "core"))
    r, c = ("x", "zh", "y"), ("zl", "core")
    in_specs = (P(None, None, r, c), P(None, r, c), P(c, None))
    return jax.shard_map(local, mesh=fine, in_specs=in_specs, out_specs=P(r, c), check_vma=False)
```

```python
import jax
import jax.numpy as jnp
from jax import lax
from jax.experimental import pallas as pl
from jax.experimental.pallas import tpu as pltpu
from jax.sharding import Mesh, PartitionSpec as P

TILE = 128
VMEM = 20 * 1024 * 1024
NT = (((1,), (1,)), ((), ()))


def halves(value):
    high = value.astype(jnp.bfloat16)
    return high, (value - high.astype(jnp.float32)).astype(jnp.bfloat16)


def dot(a, b, dims=(((1,), (0,)), ((), ()))):
    return lax.dot_general(a, b, dims, preferred_element_type=jnp.float32)


def half_kernel(half_ref, mask_ref, a_ref, c_ref, *rest):
    *o_refs, chigh, clow, ahigh, alow = rest
    chunk = pl.program_id(0)
    parts, bits, _, rows, lcols = a_ref.shape

    @pl.when(chunk == 0)
    def _():
        chigh[...], clow[...] = halves(c_ref[...])

    for p in range(parts):
        for b in range(bits):
            for j in range(lcols // TILE):
                at = (pl.ds((p * bits + b) * rows, rows), pl.ds(j * TILE, TILE))
                kept = mask_ref[p * mask_ref.shape[0] // parts, half_ref[0], j].astype(jnp.float32)
                ahigh[at], alow[at] = halves(a_ref[p, b, 0, :, at[1]] * kept)
    total = dot(ahigh[...], chigh[...]) + (dot(ahigh[...], clow[...]) + dot(alow[...], chigh[...]))
    for k, o_ref in enumerate(o_refs):
        @pl.when(chunk == k)
        def _():
            o_ref[...] = total.reshape(o_ref.shape)


def half_of(integrals, mask, coeffs, half):
    parts, mrows, lcols = integrals.shape
    norbit = coeffs.shape[1]
    rows = mrows // 8
    shape = (parts, 2, rows, norbit)
    return pl.pallas_call(
        half_kernel,
        out_shape=[jax.ShapeDtypeStruct(shape, jnp.float32)] * 2,
        grid_spec=pltpu.PrefetchScalarGridSpec(
            num_scalar_prefetch=2,
            grid=(2,),
            in_specs=[
                pl.BlockSpec((parts, 2, 1, rows, lcols), lambda k, half, mask: (0, half[0], k, 0, 0)),
                pl.BlockSpec((lcols, norbit), lambda k, half, mask: (0, 0)),
            ],
            out_specs=[pl.BlockSpec(shape, lambda k, half, mask: (0, 0, 0, 0))] * 2,
            scratch_shapes=[pltpu.VMEM((lcols, norbit), jnp.bfloat16)] * 2
            + [pltpu.VMEM((parts * 2 * rows, lcols), jnp.bfloat16)] * 2,
        ),
        compiler_params=pltpu.CompilerParams(vmem_limit_bytes=VMEM),
        cost_estimate=pl.CostEstimate(flops=3 * parts * mrows * lcols * norbit, bytes_accessed=2 * parts * mrows * (lcols + norbit) + 4 * lcols * norbit, transcendentals=0),
    )(half.reshape(1), mask, integrals.reshape(parts, 4, 2, rows, lcols), coeffs)


def exchange_kernel(core_ref, mown_ref, moth_ref, nown_ref, noth_ref, o_ref, mhigh, mlow, nhigh, nlow):
    count, rows, norbit = mown_ref.shape
    blocks, bits, nrows, _ = nown_ref.shape
    core = core_ref[0]
    both = ((core, mown_ref, nown_ref), (1 - core, moth_ref, noth_ref))

    @pl.when(pl.program_id(0) == 0)
    def _():
        for y in range(blocks):
            for c, _, ref in both:
                for b in range(bits):
                    at = pl.ds(pl.multiple_of(((y * 2 + c) * bits + b) * nrows, nrows), nrows)
                    nhigh[at, :], nlow[at, :] = halves(ref[y, b])

    for x in range(count):
        for c, ref, _ in both:
            at = pl.ds(pl.multiple_of((x * 2 + c) * rows, rows), rows)
            mhigh[at, :], mlow[at, :] = halves(ref[x])
    total = dot(mhigh[...], nhigh[...], NT) + (dot(mhigh[...], nlow[...], NT) + dot(mlow[...], nhigh[...], NT))
    o_ref[...] = total.reshape(o_ref.shape)


def exchange_part(mown, moth, nown, noth, core):
    parts, rows, norbit = mown.shape
    ncols = 2 * nown.shape[0] * nown.shape[1] * nown.shape[2]
    step = parts // 2
    mspec = pl.BlockSpec((step, rows, norbit), lambda x, core: (x, 0, 0))
    nspec = pl.BlockSpec(nown.shape, lambda x, core: (0, 0, 0, 0))
    return pl.pallas_call(
        exchange_kernel,
        out_shape=jax.ShapeDtypeStruct((parts, 2, rows, ncols), jnp.float32),
        grid_spec=pltpu.PrefetchScalarGridSpec(
            num_scalar_prefetch=1,
            grid=(2,),
            in_specs=[mspec, mspec, nspec, nspec],
            out_specs=pl.BlockSpec((step, 2, rows, ncols), lambda x, core: (x, 0, 0, 0)),
            scratch_shapes=[pltpu.VMEM((step * 2 * rows, norbit), jnp.bfloat16)] * 2 + [pltpu.VMEM((ncols, norbit), jnp.bfloat16)] * 2,
        ),
        compiler_params=pltpu.CompilerParams(vmem_limit_bytes=VMEM),
        cost_estimate=pl.CostEstimate(flops=12 * parts * rows * ncols * norbit, bytes_accessed=4 * norbit * (2 * parts * rows + ncols) + 8 * parts * rows * ncols, transcendentals=0),
    )(core.reshape(1), mown, moth, nown, noth)


def swap(value, axis, bit, size):
    return lax.ppermute(value, axis, [(i, i ^ bit) for i in range(size)])


def pick(value, index, axis):
    return lax.dynamic_index_in_dim(value, index, axis, keepdims=False)


def join(own, got, bit, axis):
    return jnp.stack([jnp.where(bit == 0, own, got), jnp.where(bit == 0, got, own)], axis=axis)


def to_x(value):
    return lax.all_to_all(value, "x", split_axis=0, concat_axis=0)


NEAR = [(z, (z + 8) % 16 if z % 2 == z // 8 else z ^ 1) for z in range(16)]
FAR = [(z, (z ^ 1) ^ 8) for z in range(16) if z % 2 != z // 8]


def local(integrals, mask, coeffs):
    nslab, naux, mrows, lcols = integrals.shape
    norbit = coeffs.shape[1]
    core, zl, zh = lax.axis_index("core"), lax.axis_index("zl"), lax.axis_index("zh")
    low, mid, top = zl & 1, (zl >> 1) & 1, zl >> 2
    parts, rows = nslab * naux, mrows // 8
    integrals = integrals.reshape(parts, mrows, lcols)
    away = half_of(integrals, mask, coeffs, 1 - core)
    got = [swap(a, "core", 1, 2) for a in away]
    kept = half_of(integrals, mask, coeffs, core)
    own = []
    for k, g in zip(kept, got):
        part = to_x(k + g)
        part = pick(part, low, 1) + swap(pick(part, 1 - low, 1), "zl", 1, 8)
        part = part.reshape(2, 2, rows, norbit)
        part = pick(part, mid, 1) + swap(pick(part, 1 - mid, 1), "zl", 2, 8)
        own.append(pick(part, top, 0) + swap(pick(part, 1 - top, 0), "zl", 4, 8))
    own = jnp.concatenate(own)
    near = lax.ppermute(own, ("zh", "zl"), NEAR)
    far = lax.ppermute(own, ("zh", "zl"), FAR)
    fits = zh == low
    cols = join(jnp.where(fits, own, near), jnp.where(fits, near, far), low, 0)
    n = lax.all_to_all(jnp.broadcast_to(cols[None], (4,) + cols.shape), "y", split_axis=0, concat_axis=0)
    n = n.reshape((2, 2) + cols.shape)
    nown, noth = pick(n, core, 0), swap(pick(n, 1 - core, 0), "core", 1, 2)
    m = join(own, swap(own, "zl", 4, 8), top, 0)
    m = join(m, swap(m, "zl", 2, 8), mid, 1).reshape(4, 2 * rows, norbit)
    tiles = []
    for m in (m, swap(m, "zl", 1, 8)):
        tile = exchange_part(m, swap(m, "core", 1, 2), nown, noth, core)
        tiles.append(jnp.sum(to_x(tile), axis=0))
    return join(*tiles, low, 1).reshape(mrows, lcols) * (1.0 / jnp.sqrt(jnp.float32(norbit * parts)))


def solution(mesh):
    fine = Mesh(mesh.devices.reshape(4, 2, 4, 8, 2), ("x", "zh", "y", "zl", "core"))
    r, c = ("x", "zh", "y"), ("zl", "core")
    in_specs = (P(None, None, r, c), P(None, r, c), P(c, None))
    return jax.shard_map(local, mesh=fine, in_specs=in_specs, out_specs=P(r, c), check_vma=False)
```

```python
import jax
import jax.numpy as jnp
from jax import lax
from jax.experimental import pallas as pl
from jax.experimental.pallas import tpu as pltpu
from jax.sharding import Mesh, PartitionSpec as P

TILE = 128
VMEM = 20 * 1024 * 1024
NT = (((1,), (1,)), ((), ()))


def halves(value):
    high = value.astype(jnp.bfloat16)
    return high, (value - high.astype(jnp.float32)).astype(jnp.bfloat16)


def dot(a, b, dims=(((1,), (0,)), ((), ()))):
    return lax.dot_general(a, b, dims, preferred_element_type=jnp.float32)


def half_kernel(half_ref, mask_ref, a_ref, c_ref, *rest):
    *o_refs, chigh, clow, ahigh, alow = rest
    chunk = pl.program_id(0)
    parts, bits, _, rows, lcols = a_ref.shape

    @pl.when(chunk == 0)
    def _():
        chigh[...], clow[...] = halves(c_ref[...])

    for p in range(parts):
        for b in range(bits):
            for j in range(lcols // TILE):
                at = (pl.ds((p * bits + b) * rows, rows), pl.ds(j * TILE, TILE))
                kept = mask_ref[p * mask_ref.shape[0] // parts, half_ref[0], j].astype(jnp.float32)
                ahigh[at], alow[at] = halves(a_ref[p, b, 0, :, at[1]] * kept)
    total = dot(ahigh[...], chigh[...]) + (dot(ahigh[...], clow[...]) + dot(alow[...], chigh[...]))
    for k, o_ref in enumerate(o_refs):
        @pl.when(chunk == k)
        def _():
            o_ref[...] = total.reshape(o_ref.shape)


def half_of(integrals, mask, coeffs, half):
    parts, mrows, lcols = integrals.shape
    norbit = coeffs.shape[1]
    rows = mrows // 8
    shape = (parts, 2, rows, norbit)
    return pl.pallas_call(
        half_kernel,
        out_shape=[jax.ShapeDtypeStruct(shape, jnp.float32)] * 2,
        grid_spec=pltpu.PrefetchScalarGridSpec(
            num_scalar_prefetch=2,
            grid=(2,),
            in_specs=[
                pl.BlockSpec((parts, 2, 1, rows, lcols), lambda k, half, mask: (0, half[0], k, 0, 0)),
                pl.BlockSpec((lcols, norbit), lambda k, half, mask: (0, 0)),
            ],
            out_specs=[pl.BlockSpec(shape, lambda k, half, mask: (0, 0, 0, 0))] * 2,
            scratch_shapes=[pltpu.VMEM((lcols, norbit), jnp.bfloat16)] * 2
            + [pltpu.VMEM((parts * 2 * rows, lcols), jnp.bfloat16)] * 2,
        ),
        compiler_params=pltpu.CompilerParams(vmem_limit_bytes=VMEM),
        cost_estimate=pl.CostEstimate(flops=3 * parts * mrows * lcols * norbit, bytes_accessed=2 * parts * mrows * (lcols + norbit) + 4 * lcols * norbit, transcendentals=0),
    )(half.reshape(1), mask, integrals.reshape(parts, 4, 2, rows, lcols), coeffs)


def exchange_kernel(core_ref, mown_ref, moth_ref, nown_ref, noth_ref, o_ref, mhigh, mlow, nhigh, nlow):
    count, rows, norbit = mown_ref.shape
    blocks, bits, nrows, _ = nown_ref.shape
    core = core_ref[0]
    both = ((core, mown_ref, nown_ref), (1 - core, moth_ref, noth_ref))

    @pl.when(pl.program_id(0) == 0)
    def _():
        for y in range(blocks):
            for c, _, ref in both:
                for b in range(bits):
                    at = pl.ds(pl.multiple_of(((y * 2 + c) * bits + b) * nrows, nrows), nrows)
                    nhigh[at, :], nlow[at, :] = halves(ref[y, b])

    for x in range(count):
        for c, ref, _ in both:
            at = pl.ds(pl.multiple_of((x * 2 + c) * rows, rows), rows)
            mhigh[at, :], mlow[at, :] = halves(ref[x])
    total = dot(mhigh[...], nhigh[...], NT) + (dot(mhigh[...], nlow[...], NT) + dot(mlow[...], nhigh[...], NT))
    o_ref[...] = total.reshape(o_ref.shape)


def exchange_part(mown, moth, nown, noth, core):
    parts, rows, norbit = mown.shape
    ncols = 2 * nown.shape[0] * nown.shape[1] * nown.shape[2]
    step = parts // 2
    mspec = pl.BlockSpec((step, rows, norbit), lambda x, core: (x, 0, 0))
    nspec = pl.BlockSpec(nown.shape, lambda x, core: (0, 0, 0, 0))
    return pl.pallas_call(
        exchange_kernel,
        out_shape=jax.ShapeDtypeStruct((parts, 2, rows, ncols), jnp.float32),
        grid_spec=pltpu.PrefetchScalarGridSpec(
            num_scalar_prefetch=1,
            grid=(2,),
            in_specs=[mspec, mspec, nspec, nspec],
            out_specs=pl.BlockSpec((step, 2, rows, ncols), lambda x, core: (x, 0, 0, 0)),
            scratch_shapes=[pltpu.VMEM((step * 2 * rows, norbit), jnp.bfloat16)] * 2 + [pltpu.VMEM((ncols, norbit), jnp.bfloat16)] * 2,
        ),
        compiler_params=pltpu.CompilerParams(vmem_limit_bytes=VMEM),
        cost_estimate=pl.CostEstimate(flops=12 * parts * rows * ncols * norbit, bytes_accessed=4 * norbit * (2 * parts * rows + ncols) + 8 * parts * rows * ncols, transcendentals=0),
    )(core.reshape(1), mown, moth, nown, noth)


def swap(value, axis, bit, size):
    return lax.ppermute(value, axis, [(i, i ^ bit) for i in range(size)])


def pick(value, index, axis):
    return lax.dynamic_index_in_dim(value, index, axis, keepdims=False)


def join(own, got, bit, axis):
    return jnp.stack([jnp.where(bit == 0, own, got), jnp.where(bit == 0, got, own)], axis=axis)


def after(value, other):
    return lax.optimization_barrier((value, other))[0]


def to_x(value):
    return lax.all_to_all(value, "x", split_axis=0, concat_axis=0)


NEAR = [(z, (z + 8) % 16 if z % 2 == z // 8 else z ^ 1) for z in range(16)]
FAR = [(z, (z ^ 1) ^ 8) for z in range(16) if z % 2 != z // 8]


def local(integrals, mask, coeffs):
    nslab, naux, mrows, lcols = integrals.shape
    norbit = coeffs.shape[1]
    core, zl, zh = lax.axis_index("core"), lax.axis_index("zl"), lax.axis_index("zh")
    low, mid, top = zl & 1, (zl >> 1) & 1, zl >> 2
    parts, rows = nslab * naux, mrows // 8
    integrals = integrals.reshape(parts, mrows, lcols)
    away = half_of(integrals, mask, coeffs, 1 - core)
    got = [swap(a, "core", 1, 2) for a in away]
    kept = half_of(integrals, mask, coeffs, core)
    own, before = [], None
    for k, g in zip(kept, got):
        give = pick(k, 1 - low, 1) + pick(g, 1 - low, 1)
        if before is not None:
            give = after(give, before)
        before = swap(give, "zl", 1, 8)
        part = to_x(pick(k, low, 1) + pick(g, low, 1) + before).reshape(2, 2, rows, norbit)
        part = pick(part, mid, 1) + swap(pick(part, 1 - mid, 1), "zl", 2, 8)
        own.append(pick(part, top, 0) + swap(pick(part, 1 - top, 0), "zl", 4, 8))
    own = jnp.concatenate(own)
    near = lax.ppermute(own, ("zh", "zl"), NEAR)
    far = lax.ppermute(own, ("zh", "zl"), FAR)
    fits = zh == low
    cols = join(jnp.where(fits, own, near), jnp.where(fits, near, far), low, 0)
    copies = jnp.broadcast_to(cols[None], (4,) + cols.shape)
    n = lax.all_to_all(copies, "y", split_axis=0, concat_axis=0)
    n = n.reshape((2, 2) + cols.shape)
    nown, noth = pick(n, core, 0), swap(pick(n, 1 - core, 0), "core", 1, 2)
    m = join(own, after(swap(own, "zl", 4, 8), copies), top, 0)
    m = join(m, swap(m, "zl", 2, 8), mid, 1).reshape(4, 2 * rows, norbit)
    tiles = []
    for m, m_swap in ((m, after(m, nown)), (swap(m, "zl", 1, 8),) * 2):
        tile = exchange_part(m, swap(m_swap, "core", 1, 2), nown, noth, core)
        tiles.append(jnp.sum(to_x(tile), axis=0))
    return join(*tiles, low, 1).reshape(mrows, lcols) * (1.0 / jnp.sqrt(jnp.float32(norbit * parts)))


def solution(mesh):
    fine = Mesh(mesh.devices.reshape(4, 2, 4, 8, 2), ("x", "zh", "y", "zl", "core"))
    r, c = ("x", "zh", "y"), ("zl", "core")
    in_specs = (P(None, None, r, c), P(None, r, c), P(c, None))
    return jax.shard_map(local, mesh=fine, in_specs=in_specs, out_specs=P(r, c), check_vma=False)
```

```python
import jax
import jax.numpy as jnp
from jax import lax
from jax.experimental import pallas as pl
from jax.experimental.pallas import tpu as pltpu
from jax.sharding import Mesh, PartitionSpec as P

TILE = 128
VMEM = 20 * 1024 * 1024
NT = (((1,), (1,)), ((), ()))


def halves(value):
    high = value.astype(jnp.bfloat16)
    return high, (value - high.astype(jnp.float32)).astype(jnp.bfloat16)


def dot(a, b, dims=(((1,), (0,)), ((), ()))):
    return lax.dot_general(a, b, dims, preferred_element_type=jnp.float32)


def half_kernel(half_ref, mask_ref, a_ref, c_ref, *rest):
    *o_refs, chigh, clow, ahigh, alow = rest
    chunk = pl.program_id(0)
    parts, bits, _, rows, lcols = a_ref.shape

    @pl.when(chunk == 0)
    def _():
        chigh[...], clow[...] = halves(c_ref[...])

    for p in range(parts):
        for b in range(bits):
            for j in range(lcols // TILE):
                at = (pl.ds((p * bits + b) * rows, rows), pl.ds(j * TILE, TILE))
                kept = mask_ref[p * mask_ref.shape[0] // parts, half_ref[0], j].astype(jnp.float32)
                ahigh[at], alow[at] = halves(a_ref[p, b, 0, :, at[1]] * kept)
    total = dot(ahigh[...], chigh[...]) + (dot(ahigh[...], clow[...]) + dot(alow[...], chigh[...]))
    for k, o_ref in enumerate(o_refs):
        @pl.when(chunk == k)
        def _():
            o_ref[...] = total.reshape(o_ref.shape)


def half_of(integrals, mask, coeffs, half, vmem):
    parts, mrows, lcols = integrals.shape
    norbit = coeffs.shape[1]
    rows = mrows // 8
    shape = (parts, 2, rows, norbit)
    return pl.pallas_call(
        half_kernel,
        out_shape=[jax.ShapeDtypeStruct(shape, jnp.float32)] * 2,
        grid_spec=pltpu.PrefetchScalarGridSpec(
            num_scalar_prefetch=2,
            grid=(2,),
            in_specs=[
                pl.BlockSpec((parts, 2, 1, rows, lcols), lambda k, half, mask: (0, half[0], k, 0, 0)),
                pl.BlockSpec((lcols, norbit), lambda k, half, mask: (0, 0)),
            ],
            out_specs=[pl.BlockSpec(shape, lambda k, half, mask: (0, 0, 0, 0))] * 2,
            scratch_shapes=[pltpu.VMEM((lcols, norbit), jnp.bfloat16)] * 2
            + [pltpu.VMEM((parts * 2 * rows, lcols), jnp.bfloat16)] * 2,
        ),
        compiler_params=pltpu.CompilerParams(vmem_limit_bytes=vmem),
        cost_estimate=pl.CostEstimate(flops=3 * parts * mrows * lcols * norbit, bytes_accessed=2 * parts * mrows * (lcols + norbit) + 4 * lcols * norbit, transcendentals=0),
    )(half.reshape(1), mask, integrals.reshape(parts, 4, 2, rows, lcols), coeffs)


def exchange_kernel(core_ref, mown_ref, moth_ref, nown_ref, noth_ref, o_ref, mhigh, mlow, nhigh, nlow):
    count, rows, norbit = mown_ref.shape
    blocks, bits, nrows, _ = nown_ref.shape
    core = core_ref[0]
    both = ((core, mown_ref, nown_ref), (1 - core, moth_ref, noth_ref))

    @pl.when(pl.program_id(0) == 0)
    def _():
        for y in range(blocks):
            for c, _, ref in both:
                for b in range(bits):
                    at = pl.ds(pl.multiple_of(((y * 2 + c) * bits + b) * nrows, nrows), nrows)
                    nhigh[at, :], nlow[at, :] = halves(ref[y, b])

    for x in range(count):
        for c, ref, _ in both:
            at = pl.ds(pl.multiple_of((x * 2 + c) * rows, rows), rows)
            mhigh[at, :], mlow[at, :] = halves(ref[x])
    total = dot(mhigh[...], nhigh[...], NT) + (dot(mhigh[...], nlow[...], NT) + dot(mlow[...], nhigh[...], NT))
    o_ref[...] = total.reshape(o_ref.shape)


def exchange_part(mown, moth, nown, noth, core):
    parts, rows, norbit = mown.shape
    ncols = 2 * nown.shape[0] * nown.shape[1] * nown.shape[2]
    step = parts // 2
    mspec = pl.BlockSpec((step, rows, norbit), lambda x, core: (x, 0, 0))
    nspec = pl.BlockSpec(nown.shape, lambda x, core: (0, 0, 0, 0))
    return pl.pallas_call(
        exchange_kernel,
        out_shape=jax.ShapeDtypeStruct((parts, 2, rows, ncols), jnp.float32),
        grid_spec=pltpu.PrefetchScalarGridSpec(
            num_scalar_prefetch=1,
            grid=(2,),
            in_specs=[mspec, mspec, nspec, nspec],
            out_specs=pl.BlockSpec((step, 2, rows, ncols), lambda x, core: (x, 0, 0, 0)),
            scratch_shapes=[pltpu.VMEM((step * 2 * rows, norbit), jnp.bfloat16)] * 2 + [pltpu.VMEM((ncols, norbit), jnp.bfloat16)] * 2,
        ),
        compiler_params=pltpu.CompilerParams(vmem_limit_bytes=VMEM),
        cost_estimate=pl.CostEstimate(flops=12 * parts * rows * ncols * norbit, bytes_accessed=4 * norbit * (2 * parts * rows + ncols) + 8 * parts * rows * ncols, transcendentals=0),
    )(core.reshape(1), mown, moth, nown, noth)


def swap(value, axis, bit, size):
    return lax.ppermute(value, axis, [(i, i ^ bit) for i in range(size)])


def pick(value, index, axis):
    return lax.dynamic_index_in_dim(value, index, axis, keepdims=False)


def join(own, got, bit, axis):
    return jnp.stack([jnp.where(bit == 0, own, got), jnp.where(bit == 0, got, own)], axis=axis)


def after(value, other):
    return lax.optimization_barrier((value, other))[0]


def to_x(value):
    return lax.all_to_all(value, "x", split_axis=0, concat_axis=0)


NEAR = [(z, (z + 8) % 16 if z % 2 == z // 8 else z ^ 1) for z in range(16)]
FAR = [(z, (z ^ 1) ^ 8) for z in range(16) if z % 2 != z // 8]


def local(integrals, mask, coeffs):
    nslab, naux, mrows, lcols = integrals.shape
    norbit = coeffs.shape[1]
    core, zl, zh = lax.axis_index("core"), lax.axis_index("zl"), lax.axis_index("zh")
    low, mid, top = zl & 1, (zl >> 1) & 1, zl >> 2
    parts, rows = nslab * naux, mrows // 8
    integrals = integrals.reshape(parts, mrows, lcols)
    away = half_of(integrals, mask, coeffs, 1 - core, 3 * VMEM)
    got = [swap(a, "core", 1, 2) for a in away]
    kept = half_of(integrals, mask, coeffs, core, VMEM)
    own, before = [], None
    for k, g in zip(kept, got):
        part = lax.optimization_barrier(k + g)
        give = pick(part, 1 - low, 1)
        if before is not None:
            give = after(give, before)
        before = swap(give, "zl", 1, 8)
        part = to_x(pick(part, low, 1) + before).reshape(2, 2, rows, norbit)
        part = pick(part, mid, 1) + swap(pick(part, 1 - mid, 1), "zl", 2, 8)
        own.append(pick(part, top, 0) + swap(pick(part, 1 - top, 0), "zl", 4, 8))
    own = jnp.concatenate(own)
    m = join(own, swap(own, "zl", 4, 8), top, 0)
    near = after(lax.ppermute(own, ("zh", "zl"), NEAR), m)
    far = after(lax.ppermute(own, ("zh", "zl"), FAR), m)
    fits = zh == low
    cols = join(jnp.where(fits, own, near), jnp.where(fits, near, far), low, 0)
    copies = jnp.broadcast_to(cols[None], (4,) + cols.shape)
    n = lax.all_to_all(copies, "y", split_axis=0, concat_axis=0)
    n = n.reshape((2, 2) + cols.shape)
    nown, noth = pick(n, core, 0), swap(pick(n, 1 - core, 0), "core", 1, 2)
    m = join(m, swap(m, "zl", 2, 8), mid, 1).reshape(4, 2 * rows, norbit)
    tiles = []
    for m, m_swap in ((m, after(m, nown)), (swap(m, "zl", 1, 8),) * 2):
        tile = exchange_part(m, swap(m_swap, "core", 1, 2), nown, noth, core)
        tiles.append(jnp.sum(to_x(tile), axis=0))
    return join(*tiles, low, 1).reshape(mrows, lcols) * (1.0 / jnp.sqrt(jnp.float32(norbit * parts)))


def solution(mesh):
    fine = Mesh(mesh.devices.reshape(4, 2, 4, 8, 2), ("x", "zh", "y", "zl", "core"))
    r, c = ("x", "zh", "y"), ("zl", "core")
    in_specs = (P(None, None, r, c), P(None, r, c), P(c, None))
    return jax.shard_map(local, mesh=fine, in_specs=in_specs, out_specs=P(r, c), check_vma=False)
```

```python
import jax
import jax.numpy as jnp
from jax import lax
from jax.experimental import pallas as pl
from jax.experimental.pallas import tpu as pltpu
from jax.sharding import Mesh, PartitionSpec as P

TILE = 128
VMEM = 20 * 1024 * 1024
NT = (((1,), (1,)), ((), ()))


def halves(value):
    high = value.astype(jnp.bfloat16)
    return high, (value - high.astype(jnp.float32)).astype(jnp.bfloat16)


def dot(a, b, dims=(((1,), (0,)), ((), ()))):
    return lax.dot_general(a, b, dims, preferred_element_type=jnp.float32)


def half_kernel(half_ref, mask_ref, a_ref, c_ref, *rest):
    *o_refs, chigh, clow, ahigh, alow = rest
    chunk = pl.program_id(0)
    parts, bits, _, rows, lcols = a_ref.shape

    @pl.when(chunk == 0)
    def _():
        chigh[...], clow[...] = halves(c_ref[...])

    for p in range(parts):
        for b in range(bits):
            for j in range(lcols // TILE):
                at = (pl.ds((p * bits + b) * rows, rows), pl.ds(j * TILE, TILE))
                kept = mask_ref[p * mask_ref.shape[0] // parts, half_ref[0], j].astype(jnp.float32)
                ahigh[at], alow[at] = halves(a_ref[p, b, 0, :, at[1]] * kept)
    total = dot(ahigh[...], chigh[...]) + (dot(ahigh[...], clow[...]) + dot(alow[...], chigh[...]))
    for k, o_ref in enumerate(o_refs):
        @pl.when(chunk == k)
        def _():
            o_ref[...] = total.reshape(o_ref.shape)


def half_of(integrals, mask, coeffs, half, vmem):
    parts, mrows, lcols = integrals.shape
    norbit = coeffs.shape[1]
    rows = mrows // 8
    shape = (parts, 2, rows, norbit)
    return pl.pallas_call(
        half_kernel,
        out_shape=[jax.ShapeDtypeStruct(shape, jnp.float32)] * 2,
        grid_spec=pltpu.PrefetchScalarGridSpec(
            num_scalar_prefetch=2,
            grid=(2,),
            in_specs=[
                pl.BlockSpec((parts, 2, 1, rows, lcols), lambda k, half, mask: (0, half[0], k, 0, 0)),
                pl.BlockSpec((lcols, norbit), lambda k, half, mask: (0, 0)),
            ],
            out_specs=[pl.BlockSpec(shape, lambda k, half, mask: (0, 0, 0, 0))] * 2,
            scratch_shapes=[pltpu.VMEM((lcols, norbit), jnp.bfloat16)] * 2
            + [pltpu.VMEM((parts * 2 * rows, lcols), jnp.bfloat16)] * 2,
        ),
        compiler_params=pltpu.CompilerParams(vmem_limit_bytes=vmem),
        cost_estimate=pl.CostEstimate(flops=3 * parts * mrows * lcols * norbit, bytes_accessed=2 * parts * mrows * (lcols + norbit) + 4 * lcols * norbit, transcendentals=0),
    )(half.reshape(1), mask, integrals.reshape(parts, 4, 2, rows, lcols), coeffs)


def exchange_kernel(core_ref, mown_ref, moth_ref, nown_ref, noth_ref, o_ref, mhigh, mlow, nhigh, nlow):
    count, rows, norbit = mown_ref.shape
    blocks, bits, nrows, _ = nown_ref.shape
    core = core_ref[0]
    both = ((core, mown_ref, nown_ref), (1 - core, moth_ref, noth_ref))

    @pl.when(pl.program_id(0) == 0)
    def _():
        for y in range(blocks):
            for c, _, ref in both:
                for b in range(bits):
                    at = pl.ds(pl.multiple_of(((y * 2 + c) * bits + b) * nrows, nrows), nrows)
                    nhigh[at, :], nlow[at, :] = halves(ref[y, b])

    for x in range(count):
        for c, ref, _ in both:
            at = pl.ds(pl.multiple_of((x * 2 + c) * rows, rows), rows)
            mhigh[at, :], mlow[at, :] = halves(ref[x])
    total = dot(mhigh[...], nhigh[...], NT) + (dot(mhigh[...], nlow[...], NT) + dot(mlow[...], nhigh[...], NT))
    o_ref[...] = total.reshape(o_ref.shape)


def exchange_part(mown, moth, nown, noth, core):
    parts, rows, norbit = mown.shape
    ncols = 2 * nown.shape[0] * nown.shape[1] * nown.shape[2]
    step = parts // 2
    mspec = pl.BlockSpec((step, rows, norbit), lambda x, core: (x, 0, 0))
    nspec = pl.BlockSpec(nown.shape, lambda x, core: (0, 0, 0, 0))
    return pl.pallas_call(
        exchange_kernel,
        out_shape=jax.ShapeDtypeStruct((parts, 2, rows, ncols), jnp.float32),
        grid_spec=pltpu.PrefetchScalarGridSpec(
            num_scalar_prefetch=1,
            grid=(2,),
            in_specs=[mspec, mspec, nspec, nspec],
            out_specs=pl.BlockSpec((step, 2, rows, ncols), lambda x, core: (x, 0, 0, 0)),
            scratch_shapes=[pltpu.VMEM((step * 2 * rows, norbit), jnp.bfloat16)] * 2 + [pltpu.VMEM((ncols, norbit), jnp.bfloat16)] * 2,
        ),
        compiler_params=pltpu.CompilerParams(vmem_limit_bytes=VMEM),
        cost_estimate=pl.CostEstimate(flops=12 * parts * rows * ncols * norbit, bytes_accessed=4 * norbit * (2 * parts * rows + ncols) + 8 * parts * rows * ncols, transcendentals=0),
    )(core.reshape(1), mown, moth, nown, noth)


def swap(value, axis, bit, size):
    return lax.ppermute(value, axis, [(i, i ^ bit) for i in range(size)])


def pick(value, index, axis):
    return lax.dynamic_index_in_dim(value, index, axis, keepdims=False)


def join(own, got, bit, axis):
    return jnp.stack([jnp.where(bit == 0, own, got), jnp.where(bit == 0, got, own)], axis=axis)


def after(value, other):
    return lax.optimization_barrier((value, other))[0]


def to_x(value):
    return lax.all_to_all(value, "x", split_axis=0, concat_axis=0)


def column_planes(z):
    half, x = z // 8, (z % 8 >> 1) ^ 1
    return half * 8 + 2 * x + half, (1 - half) * 8 + 2 * x + half


FIRST = [(z, column_planes(z)[z % 2]) for z in range(16)]
SECOND = [(z, column_planes(z)[1 - z % 2]) for z in range(16)]


def local(integrals, mask, coeffs):
    nslab, naux, mrows, lcols = integrals.shape
    norbit = coeffs.shape[1]
    core, zl, zh = lax.axis_index("core"), lax.axis_index("zl"), lax.axis_index("zh")
    low, mid, top = zl & 1, (zl >> 1) & 1, zl >> 2
    parts, rows = nslab * naux, mrows // 8
    integrals = integrals.reshape(parts, mrows, lcols)
    away = half_of(integrals, mask, coeffs, 1 - core, 3 * VMEM)
    got = [swap(a, "core", 1, 2) for a in away]
    kept = half_of(integrals, mask, coeffs, core, VMEM)
    own, before = [], None
    for k, g in zip(kept, got):
        part = lax.optimization_barrier(k + g)
        give = pick(part, 1 - low, 1)
        if before is not None:
            give = after(give, before)
        before = swap(give, "zl", 1, 8)
        part = to_x(pick(part, low, 1) + before).reshape(2, 2, rows, norbit)
        part = pick(part, 1 - mid, 1) + swap(pick(part, mid, 1), "zl", 2, 8)
        own.append(pick(part, top, 0) + swap(pick(part, 1 - top, 0), "zl", 4, 8))
    own = jnp.concatenate(own)
    m = join(own, swap(own, "zl", 4, 8), top, 0)
    first = after(lax.ppermute(own, ("zh", "zl"), FIRST), m)
    second = after(lax.ppermute(own, ("zh", "zl"), SECOND), m)
    cols = join(first, second, jnp.where(zh == low, 0, 1), 0)
    copies = jnp.broadcast_to(cols[None], (4,) + cols.shape)
    n = lax.all_to_all(copies, "y", split_axis=0, concat_axis=0)
    n = n.reshape((2, 2) + cols.shape)
    nown, noth = pick(n, core, 0), swap(pick(n, 1 - core, 0), "core", 1, 2)
    m = join(m, swap(m, "zl", 2, 8), 1 - mid, 1).reshape(4, 2 * rows, norbit)
    tiles = []
    for m, m_swap in ((m, after(m, nown)), (swap(m, "zl", 1, 8),) * 2):
        tile = exchange_part(m, swap(m_swap, "core", 1, 2), nown, noth, core)
        tiles.append(jnp.sum(to_x(tile), axis=0))
    return join(*tiles, low, 1).reshape(mrows, lcols) * (1.0 / jnp.sqrt(jnp.float32(norbit * parts)))


def solution(mesh):
    fine = Mesh(mesh.devices.reshape(4, 2, 4, 8, 2), ("x", "zh", "y", "zl", "core"))
    r, c = ("x", "zh", "y"), ("zl", "core")
    in_specs = (P(None, None, r, c), P(None, r, c), P(c, None))
    return jax.shard_map(local, mesh=fine, in_specs=in_specs, out_specs=P(r, c), check_vma=False)
```

```python
import jax
import jax.numpy as jnp
from jax import lax
from jax.experimental import pallas as pl
from jax.experimental.pallas import tpu as pltpu
from jax.sharding import Mesh, PartitionSpec as P

TILE = 128
VMEM = 20 * 1024 * 1024
NT = (((1,), (1,)), ((), ()))


def halves(value):
    high = value.astype(jnp.bfloat16)
    return high, (value - high.astype(jnp.float32)).astype(jnp.bfloat16)


def dot(a, b, dims=(((1,), (0,)), ((), ()))):
    return lax.dot_general(a, b, dims, preferred_element_type=jnp.float32)


def half_kernel(half_ref, mask_ref, a_ref, c_ref, *rest):
    *o_refs, chigh, clow, ahigh, alow = rest
    chunk = pl.program_id(0)
    parts, bits, _, rows, lcols = a_ref.shape

    @pl.when(chunk == 0)
    def _():
        chigh[...], clow[...] = halves(c_ref[...])

    for p in range(parts):
        for b in range(bits):
            for j in range(lcols // TILE):
                at = (pl.ds((p * bits + b) * rows, rows), pl.ds(j * TILE, TILE))
                kept = mask_ref[p * mask_ref.shape[0] // parts, half_ref[0], j].astype(jnp.float32)
                ahigh[at], alow[at] = halves(a_ref[p, b, 0, :, at[1]] * kept)
    total = dot(ahigh[...], chigh[...]) + (dot(ahigh[...], clow[...]) + dot(alow[...], chigh[...]))
    for k, o_ref in enumerate(o_refs):
        @pl.when(chunk == k)
        def _():
            o_ref[...] = total.reshape(o_ref.shape)


def half_of(integrals, mask, coeffs, half, vmem):
    parts, mrows, lcols = integrals.shape
    norbit = coeffs.shape[1]
    rows = mrows // 8
    shape = (parts, 2, rows, norbit)
    return pl.pallas_call(
        half_kernel,
        out_shape=[jax.ShapeDtypeStruct(shape, jnp.float32)] * 2,
        grid_spec=pltpu.PrefetchScalarGridSpec(
            num_scalar_prefetch=2,
            grid=(2,),
            in_specs=[
                pl.BlockSpec((parts, 2, 1, rows, lcols), lambda k, half, mask: (0, half[0], k, 0, 0)),
                pl.BlockSpec((lcols, norbit), lambda k, half, mask: (0, 0)),
            ],
            out_specs=[pl.BlockSpec(shape, lambda k, half, mask: (0, 0, 0, 0))] * 2,
            scratch_shapes=[pltpu.VMEM((lcols, norbit), jnp.bfloat16)] * 2
            + [pltpu.VMEM((parts * 2 * rows, lcols), jnp.bfloat16)] * 2,
        ),
        compiler_params=pltpu.CompilerParams(vmem_limit_bytes=vmem),
        cost_estimate=pl.CostEstimate(flops=3 * parts * mrows * lcols * norbit, bytes_accessed=2 * parts * mrows * (lcols + norbit) + 4 * lcols * norbit, transcendentals=0),
    )(half.reshape(1), mask, integrals.reshape(parts, 4, 2, rows, lcols), coeffs)


def exchange_kernel(core_ref, mown_ref, moth_ref, nown_ref, noth_ref, o_ref, mhigh, mlow, nhigh, nlow):
    count, rows, norbit = mown_ref.shape
    blocks, bits, nrows, _ = nown_ref.shape
    core = core_ref[0]
    both = ((core, mown_ref, nown_ref), (1 - core, moth_ref, noth_ref))

    @pl.when(pl.program_id(0) == 0)
    def _():
        for y in range(blocks):
            for c, _, ref in both:
                for b in range(bits):
                    at = pl.ds(pl.multiple_of(((y * 2 + c) * bits + b) * nrows, nrows), nrows)
                    nhigh[at, :], nlow[at, :] = halves(ref[y, b])

    for x in range(count):
        for c, ref, _ in both:
            at = pl.ds(pl.multiple_of((x * 2 + c) * rows, rows), rows)
            mhigh[at, :], mlow[at, :] = halves(ref[x])
    total = dot(mhigh[...], nhigh[...], NT) + (dot(mhigh[...], nlow[...], NT) + dot(mlow[...], nhigh[...], NT))
    o_ref[...] = total.reshape(o_ref.shape)


def exchange_part(mown, moth, nown, noth, core):
    parts, rows, norbit = mown.shape
    ncols = 2 * nown.shape[0] * nown.shape[1] * nown.shape[2]
    step = parts // 2
    mspec = pl.BlockSpec((step, rows, norbit), lambda x, core: (x, 0, 0))
    nspec = pl.BlockSpec(nown.shape, lambda x, core: (0, 0, 0, 0))
    return pl.pallas_call(
        exchange_kernel,
        out_shape=jax.ShapeDtypeStruct((parts, 2, rows, ncols), jnp.float32),
        grid_spec=pltpu.PrefetchScalarGridSpec(
            num_scalar_prefetch=1,
            grid=(2,),
            in_specs=[mspec, mspec, nspec, nspec],
            out_specs=pl.BlockSpec((step, 2, rows, ncols), lambda x, core: (x, 0, 0, 0)),
            scratch_shapes=[pltpu.VMEM((step * 2 * rows, norbit), jnp.bfloat16)] * 2 + [pltpu.VMEM((ncols, norbit), jnp.bfloat16)] * 2,
        ),
        compiler_params=pltpu.CompilerParams(vmem_limit_bytes=VMEM),
        cost_estimate=pl.CostEstimate(flops=12 * parts * rows * ncols * norbit, bytes_accessed=4 * norbit * (2 * parts * rows + ncols) + 8 * parts * rows * ncols, transcendentals=0),
    )(core.reshape(1), mown, moth, nown, noth)


def swap(value, axis, bit, size):
    return lax.ppermute(value, axis, [(i, i ^ bit) for i in range(size)])


def pick(value, index, axis):
    return lax.dynamic_index_in_dim(value, index, axis, keepdims=False)


def join(own, got, bit, axis):
    return jnp.stack([jnp.where(bit == 0, own, got), jnp.where(bit == 0, got, own)], axis=axis)


def after(value, other):
    return lax.optimization_barrier((value, other))[0]


def to_x(value):
    return lax.all_to_all(value, "x", split_axis=0, concat_axis=0)


Z = ("zh", "zq", "zb")


def column_planes(z):
    half, x = z // 8, (z % 8 >> 1) ^ 1
    return half * 8 + 2 * x + half, (1 - half) * 8 + 2 * x + half


FIRST = [(z, column_planes(z)[z % 2]) for z in range(16)]
SECOND = [(z, column_planes(z)[1 - z % 2]) for z in range(16)]


def local(integrals, mask, coeffs):
    nslab, naux, mrows, lcols = integrals.shape
    norbit = coeffs.shape[1]
    core, zq, zh = lax.axis_index("core"), lax.axis_index("zq"), lax.axis_index("zh")
    low, mid, top = lax.axis_index("zb"), zq & 1, zq >> 1
    parts, rows = nslab * naux, mrows // 8
    integrals = integrals.reshape(parts, mrows, lcols)
    away = half_of(integrals, mask, coeffs, 1 - core, 3 * VMEM)
    got = [swap(a, "core", 1, 2) for a in away]
    kept = half_of(integrals, mask, coeffs, core, VMEM)
    own = []
    for k, g in zip(kept, got):
        part = (k + g).reshape(2 * parts, rows, norbit)
        part = lax.all_to_all(part, ("x", "zb"), split_axis=0, concat_axis=0).reshape(2, 2, 2, rows, norbit)
        part = part[:, :, 0] + part[:, :, 1]
        part = pick(part, 1 - mid, 1) + swap(pick(part, mid, 1), "zq", 1, 4)
        own.append(pick(part, top, 0) + swap(pick(part, 1 - top, 0), "zq", 2, 4))
    own = jnp.concatenate(own)
    m = join(own, swap(own, "zq", 2, 4), top, 0)
    first = after(lax.ppermute(own, Z, FIRST), m)
    second = after(lax.ppermute(own, Z, SECOND), m)
    cols = join(first, second, jnp.where(zh == low, 0, 1), 0)
    copies = jnp.broadcast_to(cols[None], (4,) + cols.shape)
    n = lax.all_to_all(copies, "y", split_axis=0, concat_axis=0)
    n = n.reshape((2, 2) + cols.shape)
    nown, noth = pick(n, core, 0), swap(pick(n, 1 - core, 0), "core", 1, 2)
    m = join(m, swap(m, "zq", 1, 4), 1 - mid, 1).reshape(4, 2 * rows, norbit)
    tiles = []
    for m, m_swap in ((m, after(m, nown)), (swap(m, "zb", 1, 2),) * 2):
        tile = exchange_part(m, swap(m_swap, "core", 1, 2), nown, noth, core)
        tiles.append(jnp.sum(to_x(tile), axis=0))
    return join(*tiles, low, 1).reshape(mrows, lcols) * (1.0 / jnp.sqrt(jnp.float32(norbit * parts)))


def solution(mesh):
    fine = Mesh(mesh.devices.reshape(4, 2, 4, 4, 2, 2), ("x", "zh", "y", "zq", "zb", "core"))
    r, c = ("x", "zh", "y"), ("zq", "zb", "core")
    in_specs = (P(None, None, r, c), P(None, r, c), P(c, None))
    return jax.shard_map(local, mesh=fine, in_specs=in_specs, out_specs=P(r, c), check_vma=False)
```

```python
import jax
import jax.numpy as jnp
from jax import lax
from jax.experimental import pallas as pl
from jax.experimental.pallas import tpu as pltpu
from jax.sharding import Mesh, PartitionSpec as P

TILE = 128
VMEM = 20 * 1024 * 1024
NT = (((1,), (1,)), ((), ()))


def halves(value):
    high = value.astype(jnp.bfloat16)
    return high, (value - high.astype(jnp.float32)).astype(jnp.bfloat16)


def dot(a, b, dims=(((1,), (0,)), ((), ()))):
    return lax.dot_general(a, b, dims, preferred_element_type=jnp.float32)


def half_kernel(half_ref, mask_ref, a_ref, c_ref, *rest):
    *o_refs, chigh, clow, ahigh, alow = rest
    chunk = pl.program_id(0)
    parts, bits, _, rows, lcols = a_ref.shape

    @pl.when(chunk == 0)
    def _():
        chigh[...], clow[...] = halves(c_ref[...])

    for p in range(parts):
        for b in range(bits):
            for j in range(lcols // TILE):
                at = (pl.ds((p * bits + b) * rows, rows), pl.ds(j * TILE, TILE))
                kept = mask_ref[p * mask_ref.shape[0] // parts, half_ref[0], j].astype(jnp.float32)
                ahigh[at], alow[at] = halves(a_ref[p, b, 0, :, at[1]] * kept)
    total = dot(ahigh[...], chigh[...]) + (dot(ahigh[...], clow[...]) + dot(alow[...], chigh[...]))
    for k, o_ref in enumerate(o_refs):
        @pl.when(chunk == k)
        def _():
            o_ref[...] = total.reshape(o_ref.shape)


def half_of(integrals, mask, coeffs, half, vmem):
    parts, mrows, lcols = integrals.shape
    norbit = coeffs.shape[1]
    rows = mrows // 8
    shape = (parts, 2, rows, norbit)
    return pl.pallas_call(
        half_kernel,
        out_shape=[jax.ShapeDtypeStruct(shape, jnp.float32)] * 2,
        grid_spec=pltpu.PrefetchScalarGridSpec(
            num_scalar_prefetch=2,
            grid=(2,),
            in_specs=[
                pl.BlockSpec((parts, 2, 1, rows, lcols), lambda k, half, mask: (0, half[0], k, 0, 0)),
                pl.BlockSpec((lcols, norbit), lambda k, half, mask: (0, 0)),
            ],
            out_specs=[pl.BlockSpec(shape, lambda k, half, mask: (0, 0, 0, 0))] * 2,
            scratch_shapes=[pltpu.VMEM((lcols, norbit), jnp.bfloat16)] * 2
            + [pltpu.VMEM((parts * 2 * rows, lcols), jnp.bfloat16)] * 2,
        ),
        compiler_params=pltpu.CompilerParams(vmem_limit_bytes=vmem),
        cost_estimate=pl.CostEstimate(flops=3 * parts * mrows * lcols * norbit, bytes_accessed=2 * parts * mrows * (lcols + norbit) + 4 * lcols * norbit, transcendentals=0),
    )(half.reshape(1), mask, integrals.reshape(parts, 4, 2, rows, lcols), coeffs)


def exchange_kernel(place_ref, mown_ref, moth_ref, fown_ref, foth_ref, nown_ref, noth_ref, o_ref, mhigh, mlow, nhigh, nlow):
    count, rows, norbit = mown_ref.shape
    blocks, bits, nrows, _ = nown_ref.shape
    core, low = place_ref[0], place_ref[1]

    @pl.when(pl.program_id(0) == 0)
    def _():
        for y in range(blocks):
            for c, ref in ((core, nown_ref), (1 - core, noth_ref)):
                for b in range(bits):
                    at = pl.ds(pl.multiple_of(((y * 2 + c) * bits + b) * nrows, nrows), nrows)
                    nhigh[at, :], nlow[at, :] = halves(ref[y, b])

    for x in range(count):
        for b, own_ref, oth_ref in ((low, mown_ref, moth_ref), (1 - low, fown_ref, foth_ref)):
            for c, ref in ((core, own_ref), (1 - core, oth_ref)):
                at = pl.ds(pl.multiple_of(((x * 2 + c) * 2 + b) * rows, rows), rows)
                mhigh[at, :], mlow[at, :] = halves(ref[x])
    total = dot(mhigh[...], nhigh[...], NT) + (dot(mhigh[...], nlow[...], NT) + dot(mlow[...], nhigh[...], NT))
    o_ref[...] = total.reshape(o_ref.shape)


def exchange_part(near, far, cols, place):
    parts, rows, norbit = near[0].shape
    blocks, bits, nrows, _ = cols[0].shape
    ncols = 2 * blocks * bits * nrows
    step = parts // 2
    mspec = pl.BlockSpec((step, rows, norbit), lambda x, place: (x, 0, 0))
    nspec = pl.BlockSpec(cols[0].shape, lambda x, place: (0, 0, 0, 0))
    return pl.pallas_call(
        exchange_kernel,
        out_shape=jax.ShapeDtypeStruct((parts, 4 * rows, ncols), jnp.float32),
        grid_spec=pltpu.PrefetchScalarGridSpec(
            num_scalar_prefetch=1,
            grid=(2,),
            in_specs=[mspec] * 4 + [nspec] * 2,
            out_specs=pl.BlockSpec((step, 4 * rows, ncols), lambda x, place: (x, 0, 0)),
            scratch_shapes=[pltpu.VMEM((step * 4 * rows, norbit), jnp.bfloat16)] * 2 + [pltpu.VMEM((ncols, norbit), jnp.bfloat16)] * 2,
        ),
        compiler_params=pltpu.CompilerParams(vmem_limit_bytes=VMEM),
        cost_estimate=pl.CostEstimate(flops=24 * parts * rows * ncols * norbit, bytes_accessed=4 * norbit * (4 * parts * rows + ncols) + 16 * parts * rows * ncols, transcendentals=0),
    )(place, *near, *far, *cols)


def swap(value, axis, bit, size):
    return lax.ppermute(value, axis, [(i, i ^ bit) for i in range(size)])


def pick(value, index, axis):
    return lax.dynamic_index_in_dim(value, index, axis, keepdims=False)


def join(own, got, bit, axis):
    return jnp.stack([jnp.where(bit == 0, own, got), jnp.where(bit == 0, got, own)], axis=axis)


def after(value, other):
    return lax.optimization_barrier((value, other))[0]


def to_x(value):
    return lax.all_to_all(value, "x", split_axis=0, concat_axis=0)


Z = ("zh", "zq", "zb")


def column_planes(z):
    half, x = z // 8, (z % 8 >> 1) ^ 1
    return half * 8 + 2 * x + half, (1 - half) * 8 + 2 * x + half


FIRST = [(z, column_planes(z)[z % 2]) for z in range(16)]
SECOND = [(z, column_planes(z)[1 - z % 2]) for z in range(16)]


def local(integrals, mask, coeffs):
    nslab, naux, mrows, lcols = integrals.shape
    norbit = coeffs.shape[1]
    core, zq, zh = lax.axis_index("core"), lax.axis_index("zq"), lax.axis_index("zh")
    low, mid, top = lax.axis_index("zb"), zq & 1, zq >> 1
    parts, rows = nslab * naux, mrows // 8
    integrals = integrals.reshape(parts, mrows, lcols)
    away = half_of(integrals, mask, coeffs, 1 - core, 3 * VMEM)
    got = [swap(a, "core", 1, 2) for a in away]
    kept = half_of(integrals, mask, coeffs, core, VMEM)
    own = []
    for k, g in zip(kept, got):
        part = (k + g).reshape(2 * parts, rows, norbit)
        part = lax.all_to_all(part, ("x", "zb"), split_axis=0, concat_axis=0).reshape(2, 2, 2, rows, norbit)
        part = part[:, :, 0] + part[:, :, 1]
        part = pick(part, 1 - mid, 1) + swap(pick(part, mid, 1), "zq", 1, 4)
        own.append(pick(part, top, 0) + swap(pick(part, 1 - top, 0), "zq", 2, 4))
    own = jnp.concatenate(own)
    first = lax.ppermute(own, Z, FIRST)
    second = lax.ppermute(own, Z, SECOND)
    m = join(own, swap(own, "zq", 2, 4), top, 0)
    m = join(m, swap(m, "zq", 1, 4), 1 - mid, 1).reshape(4, 2 * rows, norbit)
    far = swap(m, "zb", 1, 2)
    cols = join(first, second, jnp.where(zh == low, 0, 1), 0)
    n = lax.all_to_all(jnp.broadcast_to(cols[None], (4,) + cols.shape), "y", split_axis=0, concat_axis=0)
    n = after(n, far).reshape((2, 2) + cols.shape)
    cols = pick(n, core, 0), swap(pick(n, 1 - core, 0), "core", 1, 2)
    near, far = (m, swap(m, "core", 1, 2)), (far, swap(far, "core", 1, 2))
    partial = to_x(exchange_part(near, far, cols, jnp.stack([core, low])))
    return jnp.sum(partial, axis=0) * (1.0 / jnp.sqrt(jnp.float32(norbit * parts)))


def solution(mesh):
    fine = Mesh(mesh.devices.reshape(4, 2, 4, 4, 2, 2), ("x", "zh", "y", "zq", "zb", "core"))
    r, c = ("x", "zh", "y"), ("zq", "zb", "core")
    in_specs = (P(None, None, r, c), P(None, r, c), P(c, None))
    return jax.shard_map(local, mesh=fine, in_specs=in_specs, out_specs=P(r, c), check_vma=False)
```

```python
import jax
import jax.numpy as jnp
from jax import lax
from jax.experimental import pallas as pl
from jax.experimental.pallas import tpu as pltpu
from jax.sharding import Mesh, PartitionSpec as P

TILE = 128
VMEM = 20 * 1024 * 1024
NT = (((1,), (1,)), ((), ()))


def halves(value):
    high = value.astype(jnp.bfloat16)
    return high, (value - high.astype(jnp.float32)).astype(jnp.bfloat16)


def dot(a, b, dims=(((1,), (0,)), ((), ()))):
    return lax.dot_general(a, b, dims, preferred_element_type=jnp.float32)


def half_kernel(half_ref, mask_ref, a_ref, c_ref, *rest):
    *o_refs, chigh, clow, ahigh, alow = rest
    chunk = pl.program_id(0)
    parts, bits, _, rows, lcols = a_ref.shape

    @pl.when(chunk == 0)
    def _():
        chigh[...], clow[...] = halves(c_ref[...])

    for p in range(parts):
        for b in range(bits):
            for j in range(lcols // TILE):
                at = (pl.ds((p * bits + b) * rows, rows), pl.ds(j * TILE, TILE))
                kept = mask_ref[p * mask_ref.shape[0] // parts, half_ref[0], j].astype(jnp.float32)
                ahigh[at], alow[at] = halves(a_ref[p, b, 0, :, at[1]] * kept)
    total = dot(ahigh[...], chigh[...]) + (dot(ahigh[...], clow[...]) + dot(alow[...], chigh[...]))
    for k, o_ref in enumerate(o_refs):
        @pl.when(chunk == k)
        def _():
            o_ref[...] = total.reshape(o_ref.shape)


def half_of(integrals, mask, coeffs, half, vmem):
    parts, mrows, lcols = integrals.shape
    norbit = coeffs.shape[1]
    rows = mrows // 8
    shape = (parts, 2, rows, norbit)
    return pl.pallas_call(
        half_kernel,
        out_shape=[jax.ShapeDtypeStruct(shape, jnp.float32)] * 2,
        grid_spec=pltpu.PrefetchScalarGridSpec(
            num_scalar_prefetch=2,
            grid=(2,),
            in_specs=[
                pl.BlockSpec((parts, 2, 1, rows, lcols), lambda k, half, mask: (0, half[0], k, 0, 0)),
                pl.BlockSpec((lcols, norbit), lambda k, half, mask: (0, 0)),
            ],
            out_specs=[pl.BlockSpec(shape, lambda k, half, mask: (0, 0, 0, 0))] * 2,
            scratch_shapes=[pltpu.VMEM((lcols, norbit), jnp.bfloat16)] * 2
            + [pltpu.VMEM((parts * 2 * rows, lcols), jnp.bfloat16)] * 2,
        ),
        compiler_params=pltpu.CompilerParams(vmem_limit_bytes=vmem),
        cost_estimate=pl.CostEstimate(flops=3 * parts * mrows * lcols * norbit, bytes_accessed=2 * parts * mrows * (lcols + norbit) + 4 * lcols * norbit, transcendentals=0),
    )(half.reshape(1), mask, integrals.reshape(parts, 4, 2, rows, lcols), coeffs)


def exchange_kernel(place_ref, mown_ref, moth_ref, fown_ref, foth_ref, nown_ref, noth_ref, o_ref, mhigh, mlow, nhigh, nlow):
    count, rows, norbit = mown_ref.shape
    blocks, bits, nrows, _ = nown_ref.shape
    core, low = place_ref[0], place_ref[1]

    @pl.when(pl.program_id(0) == 0)
    def _():
        for y in range(blocks):
            for c, ref in ((core, nown_ref), (1 - core, noth_ref)):
                for b in range(bits):
                    at = pl.ds(pl.multiple_of(((y * 2 + c) * bits + b) * nrows, nrows), nrows)
                    nhigh[at, :], nlow[at, :] = halves(ref[y, b])

    for x in range(count):
        for b, own_ref, oth_ref in ((low, mown_ref, moth_ref), (1 - low, fown_ref, foth_ref)):
            for c, ref in ((core, own_ref), (1 - core, oth_ref)):
                at = pl.ds(pl.multiple_of(((x * 2 + c) * 2 + b) * rows, rows), rows)
                mhigh[at, :], mlow[at, :] = halves(ref[x])
    total = dot(mhigh[...], nhigh[...], NT) + (dot(mhigh[...], nlow[...], NT) + dot(mlow[...], nhigh[...], NT))
    o_ref[...] = total.reshape(o_ref.shape)


def exchange_part(near, far, cols, place, shifts):
    _, rows, norbit = near[0].shape
    blocks, bits, nrows, _ = cols[0].shape
    ncols, count = 2 * blocks * bits * nrows, len(shifts)
    here = lax.axis_index("x")
    place = jnp.stack(place + [(here + shift) % 4 for shift in shifts])
    mspec = pl.BlockSpec((1, rows, norbit), lambda g, place: (place[2 + g], 0, 0))
    nspec = pl.BlockSpec(cols[0].shape, lambda g, place: (0, 0, 0, 0))
    return pl.pallas_call(
        exchange_kernel,
        out_shape=jax.ShapeDtypeStruct((count, 4 * rows, ncols), jnp.float32),
        grid_spec=pltpu.PrefetchScalarGridSpec(
            num_scalar_prefetch=1,
            grid=(count,),
            in_specs=[mspec] * 4 + [nspec] * 2,
            out_specs=pl.BlockSpec((1, 4 * rows, ncols), lambda g, place: (g, 0, 0)),
            scratch_shapes=[pltpu.VMEM((4 * rows, norbit), jnp.bfloat16)] * 2 + [pltpu.VMEM((ncols, norbit), jnp.bfloat16)] * 2,
        ),
        compiler_params=pltpu.CompilerParams(vmem_limit_bytes=VMEM),
        cost_estimate=pl.CostEstimate(flops=24 * count * rows * ncols * norbit, bytes_accessed=4 * norbit * (4 * count * rows + ncols) + 16 * count * rows * ncols, transcendentals=0),
    )(place, *near, *far, *cols)


def swap(value, axis, bit, size):
    return lax.ppermute(value, axis, [(i, i ^ bit) for i in range(size)])


def pick(value, index, axis):
    return lax.dynamic_index_in_dim(value, index, axis, keepdims=False)


def join(own, got, bit, axis):
    return jnp.stack([jnp.where(bit == 0, own, got), jnp.where(bit == 0, got, own)], axis=axis)


def after(value, other):
    return lax.optimization_barrier((value, other))[0]


def turn(value, by):
    return lax.ppermute(value, "x", [(i, (i + by) % 4) for i in range(4)])


Z = ("zh", "zq", "zb")


def column_planes(z):
    half, x = z // 8, (z % 8 >> 1) ^ 1
    return half * 8 + 2 * x + half, (1 - half) * 8 + 2 * x + half


FIRST = [(z, column_planes(z)[z % 2]) for z in range(16)]
SECOND = [(z, column_planes(z)[1 - z % 2]) for z in range(16)]


def local(integrals, mask, coeffs):
    nslab, naux, mrows, lcols = integrals.shape
    norbit = coeffs.shape[1]
    core, zq, zh = lax.axis_index("core"), lax.axis_index("zq"), lax.axis_index("zh")
    low, mid, top = lax.axis_index("zb"), zq & 1, zq >> 1
    parts, rows = nslab * naux, mrows // 8
    integrals = integrals.reshape(parts, mrows, lcols)
    away = half_of(integrals, mask, coeffs, 1 - core, 3 * VMEM)
    got = [swap(a, "core", 1, 2) for a in away]
    kept = half_of(integrals, mask, coeffs, core, VMEM)
    own = []
    for k, g in zip(kept, got):
        part = (k + g).reshape(2 * parts, rows, norbit)
        part = lax.all_to_all(part, ("x", "zb"), split_axis=0, concat_axis=0).reshape(2, 2, 2, rows, norbit)
        part = part[:, :, 0] + part[:, :, 1]
        part = pick(part, 1 - mid, 1) + swap(pick(part, mid, 1), "zq", 1, 4)
        own.append(pick(part, top, 0) + swap(pick(part, 1 - top, 0), "zq", 2, 4))
    own = jnp.concatenate(own)
    first = lax.ppermute(own, Z, FIRST)
    second = lax.ppermute(own, Z, SECOND)
    m = join(own, swap(own, "zq", 2, 4), top, 0)
    m = join(m, swap(m, "zq", 1, 4), 1 - mid, 1).reshape(4, 2 * rows, norbit)
    far = swap(m, "zb", 1, 2)
    cols = join(first, second, jnp.where(zh == low, 0, 1), 0)
    n = lax.all_to_all(jnp.broadcast_to(cols[None], (4,) + cols.shape), "y", split_axis=0, concat_axis=0)
    n = after(n, far).reshape((2, 2) + cols.shape)
    cols = pick(n, core, 0), swap(pick(n, 1 - core, 0), "core", 1, 2)
    near, far = (m, swap(m, "core", 1, 2)), (far, swap(far, "core", 1, 2))
    across = exchange_part(near, far, cols, [core, low], (2,))[0]
    half = mrows // 2
    up, down = turn(across[:half], 1), turn(across[half:], 3)
    right, left, here = exchange_part(near, far, cols, [core, low], (1, 3, 0))
    right = turn(jnp.concatenate([right[:half] + up, right[half:]]), 1)
    left = turn(jnp.concatenate([left[:half], left[half:] + down]), 3)
    return (here + right + left) * (1.0 / jnp.sqrt(jnp.float32(norbit * parts)))


def solution(mesh):
    fine = Mesh(mesh.devices.reshape(4, 2, 4, 4, 2, 2), ("x", "zh", "y", "zq", "zb", "core"))
    r, c = ("x", "zh", "y"), ("zq", "zb", "core")
    in_specs = (P(None, None, r, c), P(None, r, c), P(c, None))
    return jax.shard_map(local, mesh=fine, in_specs=in_specs, out_specs=P(r, c), check_vma=False)
```

```python
import jax
import jax.numpy as jnp
from jax import lax
from jax.experimental import pallas as pl
from jax.experimental.pallas import tpu as pltpu
from jax.sharding import Mesh, PartitionSpec as P

TILE = 128
VMEM = 20 * 1024 * 1024
NT = (((1,), (1,)), ((), ()))


def halves(value):
    high = value.astype(jnp.bfloat16)
    return high, (value - high.astype(jnp.float32)).astype(jnp.bfloat16)


def dot(a, b, dims=(((1,), (0,)), ((), ()))):
    return lax.dot_general(a, b, dims, preferred_element_type=jnp.float32)


def half_kernel(half_ref, mask_ref, a_ref, c_ref, *rest):
    *o_refs, chigh, clow, ahigh, alow = rest
    chunk = pl.program_id(0)
    parts, bits, _, rows, lcols = a_ref.shape

    @pl.when(chunk == 0)
    def _():
        chigh[...], clow[...] = halves(c_ref[...])

    for p in range(parts):
        for b in range(bits):
            for j in range(lcols // TILE):
                at = (pl.ds((p * bits + b) * rows, rows), pl.ds(j * TILE, TILE))
                kept = mask_ref[p * mask_ref.shape[0] // parts, half_ref[0], j].astype(jnp.float32)
                ahigh[at], alow[at] = halves(a_ref[p, b, 0, :, at[1]] * kept)
    total = dot(ahigh[...], chigh[...]) + (dot(ahigh[...], clow[...]) + dot(alow[...], chigh[...]))
    for k, o_ref in enumerate(o_refs):
        @pl.when(chunk == k)
        def _():
            o_ref[...] = total.reshape(o_ref.shape)


def half_of(integrals, mask, coeffs, half, vmem):
    parts, mrows, lcols = integrals.shape
    norbit = coeffs.shape[1]
    rows = mrows // 8
    shape = (parts, 2, rows, norbit)
    return pl.pallas_call(
        half_kernel,
        out_shape=[jax.ShapeDtypeStruct(shape, jnp.float32)] * 2,
        grid_spec=pltpu.PrefetchScalarGridSpec(
            num_scalar_prefetch=2,
            grid=(2,),
            in_specs=[
                pl.BlockSpec((parts, 2, 1, rows, lcols), lambda k, half, mask: (0, half[0], k, 0, 0)),
                pl.BlockSpec((lcols, norbit), lambda k, half, mask: (0, 0)),
            ],
            out_specs=[pl.BlockSpec(shape, lambda k, half, mask: (0, 0, 0, 0))] * 2,
            scratch_shapes=[pltpu.VMEM((lcols, norbit), jnp.bfloat16)] * 2
            + [pltpu.VMEM((parts * 2 * rows, lcols), jnp.bfloat16)] * 2,
        ),
        compiler_params=pltpu.CompilerParams(vmem_limit_bytes=vmem),
        cost_estimate=pl.CostEstimate(flops=3 * parts * mrows * lcols * norbit, bytes_accessed=2 * parts * mrows * (lcols + norbit) + 4 * lcols * norbit, transcendentals=0),
    )(half.reshape(1), mask, integrals.reshape(parts, 4, 2, rows, lcols), coeffs)


def exchange_kernel(place_ref, mown_ref, moth_ref, fown_ref, foth_ref, nown_ref, noth_ref, o_ref, mhigh, mlow, nhigh, nlow):
    count, rows, norbit = mown_ref.shape
    blocks, bits, nrows, _ = nown_ref.shape
    core, low = place_ref[0], place_ref[1]

    @pl.when(pl.program_id(0) == 0)
    def _():
        for y in range(blocks):
            for c, ref in ((core, nown_ref), (1 - core, noth_ref)):
                for b in range(bits):
                    at = pl.ds(pl.multiple_of(((y * 2 + c) * bits + b) * nrows, nrows), nrows)
                    nhigh[at, :], nlow[at, :] = halves(ref[y, b])

    for x in range(count):
        for b, own_ref, oth_ref in ((low, mown_ref, moth_ref), (1 - low, fown_ref, foth_ref)):
            for c, ref in ((core, own_ref), (1 - core, oth_ref)):
                at = pl.ds(pl.multiple_of(((x * 2 + c) * 2 + b) * rows, rows), rows)
                mhigh[at, :], mlow[at, :] = halves(ref[x])
    total = dot(mhigh[...], nhigh[...], NT) + (dot(mhigh[...], nlow[...], NT) + dot(mlow[...], nhigh[...], NT))
    o_ref[...] = total.reshape(o_ref.shape)


def exchange_part(near, far, cols, place):
    parts, rows, norbit = near[0].shape
    blocks, bits, nrows, _ = cols[0].shape
    ncols = 2 * blocks * bits * nrows
    step = parts // 2
    mspec = pl.BlockSpec((step, rows, norbit), lambda x, place: (x, 0, 0))
    nspec = pl.BlockSpec(cols[0].shape, lambda x, place: (0, 0, 0, 0))
    return pl.pallas_call(
        exchange_kernel,
        out_shape=jax.ShapeDtypeStruct((parts, 4 * rows, ncols), jnp.float32),
        grid_spec=pltpu.PrefetchScalarGridSpec(
            num_scalar_prefetch=1,
            grid=(2,),
            in_specs=[mspec] * 4 + [nspec] * 2,
            out_specs=pl.BlockSpec((step, 4 * rows, ncols), lambda x, place: (x, 0, 0)),
            scratch_shapes=[pltpu.VMEM((step * 4 * rows, norbit), jnp.bfloat16)] * 2 + [pltpu.VMEM((ncols, norbit), jnp.bfloat16)] * 2,
        ),
        compiler_params=pltpu.CompilerParams(vmem_limit_bytes=VMEM),
        cost_estimate=pl.CostEstimate(flops=24 * parts * rows * ncols * norbit, bytes_accessed=4 * norbit * (4 * parts * rows + ncols) + 16 * parts * rows * ncols, transcendentals=0),
    )(place, *near, *far, *cols)


def swap(value, axis, bit, size):
    return lax.ppermute(value, axis, [(i, i ^ bit) for i in range(size)])


def pick(value, index, axis):
    return lax.dynamic_index_in_dim(value, index, axis, keepdims=False)


def join(own, got, bit, axis):
    return jnp.stack([jnp.where(bit == 0, own, got), jnp.where(bit == 0, got, own)], axis=axis)


def after(value, other):
    return lax.optimization_barrier((value, other))[0]


def to_x(value):
    return lax.all_to_all(value, "x", split_axis=0, concat_axis=0)


Z = ("zh", "zq", "zb")


def column_planes(z):
    half, x = z // 8, (z % 8 >> 1) ^ 1
    return half * 8 + 2 * x + half, (1 - half) * 8 + 2 * x + half


FIRST = [(z, column_planes(z)[z % 2]) for z in range(16)]
SECOND = [(z, column_planes(z)[1 - z % 2]) for z in range(16)]


def local(integrals, mask, coeffs):
    nslab, naux, mrows, lcols = integrals.shape
    norbit = coeffs.shape[1]
    core, zq, zh = lax.axis_index("core"), lax.axis_index("zq"), lax.axis_index("zh")
    low, mid, top = lax.axis_index("zb"), zq & 1, zq >> 1
    parts, rows = nslab * naux, mrows // 8
    integrals = integrals.reshape(parts, mrows, lcols)
    away = half_of(integrals, mask, coeffs, 1 - core, 3 * VMEM)
    got = [swap(a, "core", 1, 2) for a in away]
    kept = half_of(integrals, mask, coeffs, core, VMEM)
    own = []
    for k, g in zip(kept, got):
        part = (k + g).reshape(2 * parts, rows, norbit)
        part = lax.all_to_all(part, ("x", "zb"), split_axis=0, concat_axis=0).reshape(2, 2, 2, rows, norbit)
        part = part[:, :, 0] + part[:, :, 1]
        part = pick(part, 1 - mid, 1) + swap(pick(part, mid, 1), "zq", 1, 4)
        own.append(pick(part, top, 0) + swap(pick(part, 1 - top, 0), "zq", 2, 4))
    own = jnp.concatenate(own)
    first = lax.ppermute(own, Z, FIRST)
    second = lax.ppermute(own, Z, SECOND)
    m = join(own, swap(own, "zq", 2, 4), top, 0)
    m = join(m, swap(m, "zq", 1, 4), 1 - mid, 1).reshape(4, 2 * rows, norbit)
    far = swap(m, "zb", 1, 2)
    cols = join(first, second, jnp.where(zh == low, 0, 1), 0)
    n = lax.all_to_all(jnp.broadcast_to(cols[None], (4,) + cols.shape), "y", split_axis=0, concat_axis=0)
    n = n.reshape((2, 2) + cols.shape)
    cols = pick(n, core, 0), swap(pick(n, 1 - core, 0), "core", 1, 2)
    near, far = (m, swap(m, "core", 1, 2)), (far, swap(far, "core", 1, 2))
    partial = to_x(exchange_part(near, far, cols, jnp.stack([core, low])))
    return jnp.sum(partial, axis=0) * (1.0 / jnp.sqrt(jnp.float32(norbit * parts)))


def solution(mesh):
    fine = Mesh(mesh.devices.reshape(4, 2, 4, 4, 2, 2), ("x", "zh", "y", "zq", "zb", "core"))
    r, c = ("x", "zh", "y"), ("zq", "zb", "core")
    in_specs = (P(None, None, r, c), P(None, r, c), P(c, None))
    return jax.shard_map(local, mesh=fine, in_specs=in_specs, out_specs=P(r, c), check_vma=False)
```

```python
import jax
import jax.numpy as jnp
from jax import lax
from jax.experimental import pallas as pl
from jax.experimental.pallas import tpu as pltpu
from jax.sharding import Mesh, PartitionSpec as P

TILE = 128
VMEM = 20 * 1024 * 1024
NT = (((1,), (1,)), ((), ()))


def halves(value):
    high = value.astype(jnp.bfloat16)
    return high, (value - high.astype(jnp.float32)).astype(jnp.bfloat16)


def dot(a, b, dims=(((1,), (0,)), ((), ()))):
    return lax.dot_general(a, b, dims, preferred_element_type=jnp.float32)


def half_kernel(half_ref, mask_ref, a_ref, c_ref, *rest):
    *o_refs, chigh, clow, ahigh, alow = rest
    chunk = pl.program_id(0)
    parts, bits, _, rows, lcols = a_ref.shape

    @pl.when(chunk == 0)
    def _():
        chigh[...], clow[...] = halves(c_ref[...])

    for p in range(parts):
        for b in range(bits):
            for j in range(lcols // TILE):
                at = (pl.ds((p * bits + b) * rows, rows), pl.ds(j * TILE, TILE))
                kept = mask_ref[p * mask_ref.shape[0] // parts, half_ref[0], j].astype(jnp.float32)
                ahigh[at], alow[at] = halves(a_ref[p, b, 0, :, at[1]] * kept)
    total = dot(ahigh[...], chigh[...]) + (dot(ahigh[...], clow[...]) + dot(alow[...], chigh[...]))
    for k, o_ref in enumerate(o_refs):
        @pl.when(chunk == k)
        def _():
            o_ref[...] = total.reshape(o_ref.shape)


def half_of(integrals, mask, coeffs, half, vmem):
    parts, mrows, lcols = integrals.shape
    norbit = coeffs.shape[1]
    rows = mrows // 8
    shape = (parts, 2, rows, norbit)
    return pl.pallas_call(
        half_kernel,
        out_shape=[jax.ShapeDtypeStruct(shape, jnp.float32)] * 2,
        grid_spec=pltpu.PrefetchScalarGridSpec(
            num_scalar_prefetch=2,
            grid=(2,),
            in_specs=[
                pl.BlockSpec((parts, 2, 1, rows, lcols), lambda k, half, mask: (0, half[0], k, 0, 0)),
                pl.BlockSpec((lcols, norbit), lambda k, half, mask: (0, 0)),
            ],
            out_specs=[pl.BlockSpec(shape, lambda k, half, mask: (0, 0, 0, 0))] * 2,
            scratch_shapes=[pltpu.VMEM((lcols, norbit), jnp.bfloat16)] * 2
            + [pltpu.VMEM((parts * 2 * rows, lcols), jnp.bfloat16)] * 2,
        ),
        compiler_params=pltpu.CompilerParams(vmem_limit_bytes=vmem),
        cost_estimate=pl.CostEstimate(flops=3 * parts * mrows * lcols * norbit, bytes_accessed=2 * parts * mrows * (lcols + norbit) + 4 * lcols * norbit, transcendentals=0),
    )(half.reshape(1), mask, integrals.reshape(parts, 4, 2, rows, lcols), coeffs)


def exchange_kernel(place_ref, mown_ref, moth_ref, nown_ref, noth_ref, *rest):
    *_, o_ref, mhigh, mlow, nhigh, nlow = rest
    count, rows, norbit = mown_ref.shape
    blocks, bits, nrows, _ = nown_ref.shape
    core = place_ref[0]
    both = ((core, mown_ref, nown_ref), (1 - core, moth_ref, noth_ref))

    @pl.when(pl.program_id(0) == 0)
    def _():
        for y in range(blocks):
            for c, _, ref in both:
                for b in range(bits):
                    at = pl.ds(pl.multiple_of(((y * 2 + c) * bits + b) * nrows, nrows), nrows)
                    nhigh[at, :], nlow[at, :] = halves(ref[y, b])

    for x in range(count):
        for c, ref, _ in both:
            at = pl.ds(pl.multiple_of((x * 2 + c) * rows, rows), rows)
            mhigh[at, :], mlow[at, :] = halves(ref[x])
    total = dot(mhigh[...], nhigh[...], NT) + (dot(mhigh[...], nlow[...], NT) + dot(mlow[...], nhigh[...], NT))
    o_ref[...] = total.reshape(o_ref.shape)


def exchange_part(mown, moth, nown, noth, core, bit, before):
    parts, rows, norbit = mown.shape
    ncols = 2 * nown.shape[0] * nown.shape[1] * nown.shape[2]
    step = parts // 2
    mspec = pl.BlockSpec((step, rows, norbit), lambda x, place: (x, 0, 0))
    nspec = pl.BlockSpec(nown.shape, lambda x, place: (0, 0, 0, 0))
    return pl.pallas_call(
        exchange_kernel,
        out_shape=jax.ShapeDtypeStruct((parts, 2, 2, rows, ncols), jnp.float32),
        grid_spec=pltpu.PrefetchScalarGridSpec(
            num_scalar_prefetch=1,
            grid=(2,),
            in_specs=[mspec, mspec, nspec, nspec] + [pl.BlockSpec(memory_space=pl.ANY)] * len(before),
            out_specs=pl.BlockSpec((step, 2, 1, rows, ncols), lambda x, place: (x, 0, place[1], 0, 0)),
            scratch_shapes=[pltpu.VMEM((step * 2 * rows, norbit), jnp.bfloat16)] * 2 + [pltpu.VMEM((ncols, norbit), jnp.bfloat16)] * 2,
        ),
        input_output_aliases={5: 0} if before else {},
        compiler_params=pltpu.CompilerParams(vmem_limit_bytes=VMEM),
        cost_estimate=pl.CostEstimate(flops=12 * parts * rows * ncols * norbit, bytes_accessed=4 * norbit * (2 * parts * rows + ncols) + 8 * parts * rows * ncols, transcendentals=0),
    )(jnp.stack([core, bit]), mown, moth, nown, noth, *before)


def swap(value, axis, bit, size):
    return lax.ppermute(value, axis, [(i, i ^ bit) for i in range(size)])


def pick(value, index, axis):
    return lax.dynamic_index_in_dim(value, index, axis, keepdims=False)


def join(own, got, bit, axis):
    return jnp.stack([jnp.where(bit == 0, own, got), jnp.where(bit == 0, got, own)], axis=axis)


def after(value, other):
    return lax.optimization_barrier((value, other))[0]


def to_x(value):
    return lax.all_to_all(value, "x", split_axis=0, concat_axis=0)


Z = ("zh", "zq", "zb")


def column_planes(z):
    half, x = z // 8, (z % 8 >> 1) ^ 1
    return half * 8 + 2 * x + half, (1 - half) * 8 + 2 * x + half


FIRST = [(z, column_planes(z)[z % 2]) for z in range(16)]
SECOND = [(z, column_planes(z)[1 - z % 2]) for z in range(16)]


def local(integrals, mask, coeffs):
    nslab, naux, mrows, lcols = integrals.shape
    norbit = coeffs.shape[1]
    core, zq, zh = lax.axis_index("core"), lax.axis_index("zq"), lax.axis_index("zh")
    low, mid, top = lax.axis_index("zb"), zq & 1, zq >> 1
    parts, rows = nslab * naux, mrows // 8
    integrals = integrals.reshape(parts, mrows, lcols)
    away = half_of(integrals, mask, coeffs, 1 - core, 3 * VMEM)
    got = [swap(a, "core", 1, 2) for a in away]
    kept = half_of(integrals, mask, coeffs, core, VMEM)
    own = []
    for k, g in zip(kept, got):
        part = (k + g).reshape(2 * parts, rows, norbit)
        part = lax.all_to_all(part, ("x", "zb"), split_axis=0, concat_axis=0).reshape(2, 2, 2, rows, norbit)
        part = part[:, :, 0] + part[:, :, 1]
        part = pick(part, 1 - mid, 1) + swap(pick(part, mid, 1), "zq", 1, 4)
        own.append(pick(part, top, 0) + swap(pick(part, 1 - top, 0), "zq", 2, 4))
    own = jnp.concatenate(own)
    first = lax.ppermute(own, Z, FIRST)
    second = lax.ppermute(own, Z, SECOND)
    m = join(own, swap(own, "zq", 2, 4), top, 0)
    m = join(m, swap(m, "zq", 1, 4), 1 - mid, 1).reshape(4, 2 * rows, norbit)
    far = swap(m, "zb", 1, 2)
    cols = join(first, second, jnp.where(zh == low, 0, 1), 0)
    n = lax.all_to_all(jnp.broadcast_to(cols[None], (4,) + cols.shape), "y", split_axis=0, concat_axis=0)
    n = n.reshape((2, 2) + cols.shape)
    cols = pick(n, core, 0), swap(pick(n, 1 - core, 0), "core", 1, 2)
    tile = exchange_part(m, swap(m, "core", 1, 2), *cols, core, low, ())
    tile = exchange_part(far, swap(far, "core", 1, 2), *cols, core, 1 - low, (tile,))
    partial = to_x(tile.reshape(4, mrows, lcols))
    return jnp.sum(partial, axis=0) * (1.0 / jnp.sqrt(jnp.float32(norbit * parts)))


def solution(mesh):
    fine = Mesh(mesh.devices.reshape(4, 2, 4, 4, 2, 2), ("x", "zh", "y", "zq", "zb", "core"))
    r, c = ("x", "zh", "y"), ("zq", "zb", "core")
    in_specs = (P(None, None, r, c), P(None, r, c), P(c, None))
    return jax.shard_map(local, mesh=fine, in_specs=in_specs, out_specs=P(r, c), check_vma=False)
```

```python
import jax
import jax.numpy as jnp
from jax import lax
from jax.experimental import pallas as pl
from jax.experimental.pallas import tpu as pltpu
from jax.sharding import Mesh, PartitionSpec as P

TILE = 128
VMEM = 20 * 1024 * 1024
NT = (((1,), (1,)), ((), ()))


def halves(value):
    high = value.astype(jnp.bfloat16)
    return high, (value - high.astype(jnp.float32)).astype(jnp.bfloat16)


def dot(a, b, dims=(((1,), (0,)), ((), ()))):
    return lax.dot_general(a, b, dims, preferred_element_type=jnp.float32)


def half_kernel(half_ref, mask_ref, a_ref, c_ref, *rest):
    *o_refs, chigh, clow, ahigh, alow = rest
    chunk = pl.program_id(0)
    parts, bits, _, rows, lcols = a_ref.shape

    @pl.when(chunk == 0)
    def _():
        chigh[...], clow[...] = halves(c_ref[...])

    for p in range(parts):
        for b in range(bits):
            for j in range(lcols // TILE):
                at = (pl.ds((p * bits + b) * rows, rows), pl.ds(j * TILE, TILE))
                kept = mask_ref[p * mask_ref.shape[0] // parts, half_ref[0], j].astype(jnp.float32)
                ahigh[at], alow[at] = halves(a_ref[p, b, 0, :, at[1]] * kept)
    total = dot(ahigh[...], chigh[...]) + (dot(ahigh[...], clow[...]) + dot(alow[...], chigh[...]))
    for k, o_ref in enumerate(o_refs):
        @pl.when(chunk == k)
        def _():
            o_ref[...] = total.reshape(o_ref.shape)


def half_of(integrals, mask, coeffs, half, vmem):
    parts, mrows, lcols = integrals.shape
    norbit = coeffs.shape[1]
    rows = mrows // 8
    shape = (parts, 2, rows, norbit)
    return pl.pallas_call(
        half_kernel,
        out_shape=[jax.ShapeDtypeStruct(shape, jnp.float32)] * 2,
        grid_spec=pltpu.PrefetchScalarGridSpec(
            num_scalar_prefetch=2,
            grid=(2,),
            in_specs=[
                pl.BlockSpec((parts, 2, 1, rows, lcols), lambda k, half, mask: (0, half[0], k, 0, 0)),
                pl.BlockSpec((lcols, norbit), lambda k, half, mask: (0, 0)),
            ],
            out_specs=[pl.BlockSpec(shape, lambda k, half, mask: (0, 0, 0, 0))] * 2,
            scratch_shapes=[pltpu.VMEM((lcols, norbit), jnp.bfloat16)] * 2
            + [pltpu.VMEM((parts * 2 * rows, lcols), jnp.bfloat16)] * 2,
        ),
        compiler_params=pltpu.CompilerParams(vmem_limit_bytes=vmem),
        cost_estimate=pl.CostEstimate(flops=3 * parts * mrows * lcols * norbit, bytes_accessed=2 * parts * mrows * (lcols + norbit) + 4 * lcols * norbit, transcendentals=0),
    )(half.reshape(1), mask, integrals.reshape(parts, 4, 2, rows, lcols), coeffs)


def exchange_kernel(core_ref, mown_ref, moth_ref, nown_ref, noth_ref, o_ref, mhigh, mlow, nhigh, nlow):
    count, rows, norbit = mown_ref.shape
    blocks, bits, nrows, _ = nown_ref.shape
    core = core_ref[0]
    both = ((core, mown_ref, nown_ref), (1 - core, moth_ref, noth_ref))

    @pl.when(pl.program_id(0) == 0)
    def _():
        for y in range(blocks):
            for c, _, ref in both:
                for b in range(bits):
                    at = pl.ds(pl.multiple_of(((y * 2 + c) * bits + b) * nrows, nrows), nrows)
                    nhigh[at, :], nlow[at, :] = halves(ref[y, b])

    for x in range(count):
        for c, ref, _ in both:
            at = pl.ds(pl.multiple_of((x * 2 + c) * rows, rows), rows)
            mhigh[at, :], mlow[at, :] = halves(ref[x])
    total = dot(mhigh[...], nhigh[...], NT) + (dot(mhigh[...], nlow[...], NT) + dot(mlow[...], nhigh[...], NT))
    o_ref[...] = total.reshape(o_ref.shape)


def exchange_part(mown, moth, nown, noth, core):
    parts, rows, norbit = mown.shape
    ncols = 2 * nown.shape[0] * nown.shape[1] * nown.shape[2]
    step = parts // 2
    mspec = pl.BlockSpec((step, rows, norbit), lambda x, core: (x, 0, 0))
    nspec = pl.BlockSpec(nown.shape, lambda x, core: (0, 0, 0, 0))
    return pl.pallas_call(
        exchange_kernel,
        out_shape=jax.ShapeDtypeStruct((parts, 2, rows, ncols), jnp.float32),
        grid_spec=pltpu.PrefetchScalarGridSpec(
            num_scalar_prefetch=1,
            grid=(2,),
            in_specs=[mspec, mspec, nspec, nspec],
            out_specs=pl.BlockSpec((step, 2, rows, ncols), lambda x, core: (x, 0, 0, 0)),
            scratch_shapes=[pltpu.VMEM((step * 2 * rows, norbit), jnp.bfloat16)] * 2 + [pltpu.VMEM((ncols, norbit), jnp.bfloat16)] * 2,
        ),
        compiler_params=pltpu.CompilerParams(vmem_limit_bytes=VMEM),
        cost_estimate=pl.CostEstimate(flops=12 * parts * rows * ncols * norbit, bytes_accessed=4 * norbit * (2 * parts * rows + ncols) + 8 * parts * rows * ncols, transcendentals=0),
    )(core.reshape(1), mown, moth, nown, noth)


def swap(value, axis, bit, size):
    return lax.ppermute(value, axis, [(i, i ^ bit) for i in range(size)])


def pick(value, index, axis):
    return lax.dynamic_index_in_dim(value, index, axis, keepdims=False)


def join(own, got, bit, axis):
    return jnp.stack([jnp.where(bit == 0, own, got), jnp.where(bit == 0, got, own)], axis=axis)


def after(value, other):
    return lax.optimization_barrier((value, other))[0]


def to_x(value):
    return lax.all_to_all(value, "x", split_axis=0, concat_axis=0)


Z = ("zh", "zq", "zb")


def column_planes(z):
    half, x = z // 8, (z % 8 >> 1) ^ 1
    return half * 8 + 2 * x + half, (1 - half) * 8 + 2 * x + half


FIRST = [(z, column_planes(z)[z % 2]) for z in range(16)]
SECOND = [(z, column_planes(z)[1 - z % 2]) for z in range(16)]


def local(integrals, mask, coeffs):
    nslab, naux, mrows, lcols = integrals.shape
    norbit = coeffs.shape[1]
    core, zq, zh = lax.axis_index("core"), lax.axis_index("zq"), lax.axis_index("zh")
    low, mid, top = lax.axis_index("zb"), zq & 1, zq >> 1
    parts, rows = nslab * naux, mrows // 8
    integrals = integrals.reshape(parts, mrows, lcols)
    away = half_of(integrals, mask, coeffs, 1 - core, 3 * VMEM)
    got = [swap(a, "core", 1, 2) for a in away]
    kept = half_of(integrals, mask, coeffs, core, VMEM)
    own = []
    for k, g in zip(kept, got):
        part = (k + g).reshape(2 * parts, rows, norbit)
        part = lax.all_to_all(part, ("x", "zb"), split_axis=0, concat_axis=0).reshape(2, 2, 2, rows, norbit)
        part = part[:, :, 0] + part[:, :, 1]
        part = pick(part, 1 - mid, 1) + swap(pick(part, mid, 1), "zq", 1, 4)
        own.append(pick(part, top, 0) + swap(pick(part, 1 - top, 0), "zq", 2, 4))
    own = jnp.concatenate(own)
    m = join(own, swap(own, "zq", 2, 4), top, 0)
    first = after(lax.ppermute(own, Z, FIRST), m)
    second = after(lax.ppermute(own, Z, SECOND), m)
    cols = join(first, second, jnp.where(zh == low, 0, 1), 0)
    copies = jnp.broadcast_to(cols[None], (4,) + cols.shape)
    n = lax.all_to_all(copies, "y", split_axis=0, concat_axis=0)
    n = n.reshape((2, 2) + cols.shape)
    nown, noth = pick(n, core, 0), swap(pick(n, 1 - core, 0), "core", 1, 2)
    m = join(m, swap(m, "zq", 1, 4), 1 - mid, 1).reshape(4, 2 * rows, norbit)
    tiles = []
    for m, m_swap in ((m, m), (swap(m, "zb", 1, 2),) * 2):
        tile = exchange_part(m, swap(m_swap, "core", 1, 2), nown, noth, core)
        tiles.append(jnp.sum(to_x(tile), axis=0))
    return join(*tiles, low, 1).reshape(mrows, lcols) * (1.0 / jnp.sqrt(jnp.float32(norbit * parts)))


def solution(mesh):
    fine = Mesh(mesh.devices.reshape(4, 2, 4, 4, 2, 2), ("x", "zh", "y", "zq", "zb", "core"))
    r, c = ("x", "zh", "y"), ("zq", "zb", "core")
    in_specs = (P(None, None, r, c), P(None, r, c), P(c, None))
    return jax.shard_map(local, mesh=fine, in_specs=in_specs, out_specs=P(r, c), check_vma=False)
```
